256 devices in a mesh: ctx: 64 (over y, z, core), tp: 4 (over x).
Axes of the slice: x: 4, y: 4, z: 8, core: 2. Of those that a mesh axis runs over, the one named last changes fastest.
Arguments:
- qkv: bfloat16 [3, 16384, 4096], P(None, 'ctx', 'tp'), may hold values from -6 to 6
- short_taps: float32 [3, 3, 4096], P(None, None, 'tp'), may hold values from -3 to 3
- long_filter: bfloat16 [16384, 4096], P('ctx', 'tp'), may hold values from -0.046875 to 0.046875
- skip: float32 [4096], P('tp'), may hold values from 0.5 to 1.5
- out_weight: bfloat16 [4096, 4096], P('tp'), may hold values from -0.09375 to 0.09375
Outputs:
- mixed: bfloat16 [16384, 4096], P('ctx', 'tp')
The draws below stay inside these ranges and needn't reach their ends.
All inputs are finite; a program needn't handle non-finite values.
Results may differ from the reference program's by a relative error of at most 0.024.
Values may be sent and summed in bfloat16 or wider, within the bound.
A program may use at most 128 MiB of HBM per device.

```python
import math
import jax
import jax.numpy as jnp
from jax import lax

D = 4096
TOK_DEV = 256
SEQ = 16384
BLOCKS = 64


def block_levels(rng, extent, split, low, high):
    def one(axis_at, shards_of):
        heights = jax.random.uniform(jax.random.fold_in(jax.random.fold_in(rng, 6), axis_at), (shards_of,), jnp.float32, low / len(split), high / len(split))
        return jnp.repeat(jnp.exp(heights), extent[axis_at] // shards_of).reshape((-1,) + (1,) * (len(extent) - axis_at - 1))

    loudness = one(*split[0])
    for cut in split[1:]:
        loudness = loudness * one(*cut)
    return loudness


def centred(key, shape, scale, reach, shards=(), kind=jnp.bfloat16):
    array = jax.random.normal(key, shape, jnp.float32) * scale
    if len(shards) > 0:
        array = block_levels(key, shape, shards, -0.22, 0.18) * array
    return jnp.clip(array, min=-reach, max=reach).astype(kind)


def setup_inputs(seed: int = 0) -> dict:
    keys = jax.random.split(jax.random.key(seed), 6)
    return {
        "qkv": centred(keys[0], (3, SEQ, D), 1.0, 6.0, ((1, 64), (2, 4))),
        "short_taps": centred(keys[1], (3, 3, D), 0.6, 3.0, ((2, 4),), jnp.float32),
        "long_filter": centred(keys[2], (SEQ, D), SEQ ** -0.5, 0.046875, ((0, 64), (1, 4))),
        "skip": jnp.clip(0.5 + 1.0 * jax.random.uniform(keys[3], (D,), jnp.float32) ** block_levels(keys[3], (D,), ((0, 4),), -0.2, 0.2), 0.5, 1.5),
        "out_weight": centred(keys[4], (D, D), D ** -0.5, 0.09375, ((0, 4),)),
    }


def round_complex(value):
    real_part = lax.optimization_barrier(jnp.real(value).astype(jnp.bfloat16)).astype(jnp.float32)
    imag_part = lax.optimization_barrier(jnp.imag(value).astype(jnp.bfloat16)).astype(jnp.float32)
    return real_part + 1j * imag_part


def long_block(signal_part, filter_part):
    points = 2 * SEQ
    freqs = jnp.arange(2 * BLOCKS, dtype=jnp.int32)[:, None]
    offset = jnp.arange(TOK_DEV, dtype=jnp.int32)[None, :]
    phase = (freqs * offset) % points
    angle = phase.astype(jnp.float32) * (2.0 * math.pi / points)
    twiddle = jnp.cos(angle) - 1j * jnp.sin(angle)

    def forward(values):
        blocked = values.reshape(BLOCKS, TOK_DEV, values.shape[1])
        padded = jnp.concatenate([blocked, jnp.zeros_like(blocked)], axis=0)
        first = round_complex(jnp.fft.fft(padded, axis=0))
        return round_complex(jnp.fft.fft(first * twiddle[:, :, None], axis=1))

    product = round_complex(forward(signal_part) * forward(filter_part))
    back = round_complex(jnp.conj(twiddle)[:, :, None] * (jnp.fft.ifft(product, axis=1) * TOK_DEV))
    conv = jnp.real(jnp.fft.ifft(back, axis=0))[:BLOCKS] * (2.0 * BLOCKS / points)
    return conv.reshape(SEQ, signal_part.shape[1]).astype(jnp.bfloat16)


def reference(qkv, short_taps, long_filter, skip, out_weight):
    raw = qkv.astype(jnp.float32)
    padded = jnp.pad(raw, ((0, 0), (2, 0), (0, 0)))
    shortened = short_taps[:, 0][:, None, :] * raw + short_taps[:, 1][:, None, :] * padded[:, 1:-1] + short_taps[:, 2][:, None, :] * padded[:, :-2]
    signal = (shortened[1] * shortened[2]).astype(jnp.bfloat16)
    width = min(D, 512)
    count = D // width

    def split_blocks(values):
        return values.astype(jnp.float32).reshape(SEQ, count, width).transpose(1, 0, 2)

    conv = lax.map(lambda pair: long_block(pair[0], pair[1]), (split_blocks(signal), split_blocks(long_filter)))
    conv = conv.transpose(1, 0, 2).reshape(SEQ, D)
    gated = (shortened[0] * (conv.astype(jnp.float32) + skip * signal.astype(jnp.float32))).astype(jnp.bfloat16)
    return jnp.dot(gated, out_weight, preferred_element_type=jnp.float32).astype(jnp.bfloat16)
```

```python
import functools

import jax
import jax.numpy as jnp
import numpy as np
from jax import lax
from jax.experimental import pallas as pl
from jax.experimental.pallas import tpu as pltpu
from jax.sharding import PartitionSpec as P

GROUP = 13


def tables(blocks, width, lanes):
    freqs = blocks + 1
    points = 2 * blocks * width
    f = np.arange(freqs)
    angle = 2.0 * np.pi * np.outer(f, np.arange(blocks)) / (2 * blocks)
    steps = freqs // GROUP
    eye = np.eye(lanes)
    pair = np.stack([np.cos(angle), -np.sin(angle)]).reshape(2, steps, GROUP, blocks)
    pair = pair.transpose(1, 0, 2, 3).reshape(2 * freqs, blocks)
    lead = np.kron(pair, eye)
    weight = np.where((f == 0) | (f == blocks), 1.0, 2.0)[:, None] / points
    turn = 2.0 * np.pi * np.outer(f, np.arange(width)) / points
    twiddle = np.stack([np.cos(turn), -np.sin(turn)])
    twiddle = np.repeat(twiddle, lanes, axis=1)
    inner = 2.0 * np.pi * np.outer(np.arange(width), np.arange(width)) / width
    c, s = np.cos(inner), np.sin(inner)
    forward = np.block([[c, -s], [s, c]])
    backward = np.block([[c, s], [-s, c]])
    scaled = np.stack([np.cos(angle) * weight, -np.sin(angle) * weight]).reshape(2, steps, GROUP, blocks)
    scaled = scaled.transpose(1, 0, 2, 3).reshape(2 * freqs, blocks)
    tail = np.kron(scaled.T, eye)
    half = jnp.bfloat16
    return (
        lead.astype(half),
        tail.astype(half),
        twiddle.astype(np.float32),
        forward.astype(half),
        backward.astype(half),
    )


def dot(left, right):
    return jnp.dot(left, right, preferred_element_type=jnp.float32)


def conv_kernel(x_ref, h_ref, lead_ref, tail_ref, twiddle_ref, forward_ref, backward_ref, y_ref, back_ref, rows, steps):
    width = x_ref.shape[1]

    def step(i, carry):
        at = pl.ds(pl.multiple_of(i * rows, 16), rows)
        at2 = pl.ds(pl.multiple_of(i * 2 * rows, 16), 2 * rows)
        cos = twiddle_ref[0, at, :]
        sin = twiddle_ref[1, at, :]

        def spectrum(ref):
            first = dot(lead_ref[at2, :], ref[...])
            real, imag = first[:rows], first[rows:]
            turned = jnp.concatenate([real * cos - imag * sin, real * sin + imag * cos], axis=1)
            return dot(turned.astype(jnp.bfloat16), forward_ref[...])

        sx = spectrum(x_ref)
        sh = spectrum(h_ref)
        xr, xi = sx[:, :width], sx[:, width:]
        hr, hi = sh[:, :width], sh[:, width:]
        product = jnp.concatenate([xr * hr - xi * hi, xr * hi + xi * hr], axis=1)
        back = dot(product.astype(jnp.bfloat16), backward_ref[...])
        br, bi = back[:, :width], back[:, width:]
        out = jnp.concatenate([br * cos + bi * sin, bi * cos - br * sin], axis=0)
        back_ref[at2, :] = out.astype(jnp.bfloat16)
        return carry

    lax.fori_loop(0, steps, step, 0)
    y_ref[...] = dot(tail_ref[...], back_ref[...]).astype(jnp.bfloat16)


def long_conv(x, h):
    blocks, lanes, width = x.shape
    consts = tables(blocks, width, lanes)
    freqs = blocks + 1
    vmem = pl.BlockSpec(memory_space=pltpu.VMEM)
    out = pl.pallas_call(
        functools.partial(conv_kernel, rows=GROUP * lanes, steps=freqs // GROUP),
        out_shape=jax.ShapeDtypeStruct((blocks * lanes, width), jnp.bfloat16),
        in_specs=[vmem] * 7,
        out_specs=vmem,
        scratch_shapes=[pltpu.VMEM((2 * freqs * lanes, width), jnp.bfloat16)],
        compiler_params=pltpu.CompilerParams(vmem_limit_bytes=48 << 20),
    )(x.reshape(blocks * lanes, width), h.reshape(blocks * lanes, width), *[jnp.asarray(c) for c in consts])
    return out.reshape(blocks, lanes, width)


def body(qkv, short_taps, long_filter, skip, out_weight):
    f32 = jnp.float32
    blocks = lax.axis_size("ctx")
    tokens, channels = qkv.shape[1:]
    lanes = channels // blocks
    edge = lax.ppermute(qkv[:, tokens - 2 :, :], "ctx", [(i, i + 1) for i in range(blocks - 1)])
    padded = jnp.concatenate([edge, qkv], axis=1).astype(f32)
    shortened = (
        short_taps[:, 0][:, None, :] * padded[:, 2:]
        + short_taps[:, 1][:, None, :] * padded[:, 1:-1]
        + short_taps[:, 2][:, None, :] * padded[:, :-2]
    )
    signal = (shortened[1] * shortened[2]).astype(jnp.bfloat16)

    def exchange(value):
        return lax.all_to_all(value.reshape(blocks, lanes, tokens), "ctx", split_axis=0, concat_axis=0, tiled=True)

    taps = exchange(long_filter.T)
    spread = exchange(signal.T)
    conv = exchange(long_conv(spread, taps)).reshape(channels, tokens).T
    gated = (shortened[0] * (conv.astype(f32) + skip * signal.astype(f32))).astype(jnp.bfloat16)
    terms = jnp.dot(gated, out_weight, preferred_element_type=f32)
    return lax.psum_scatter(terms.astype(jnp.bfloat16), "tp", scatter_dimension=1, tiled=True)


def solution(mesh):
    placed = (P(None, "ctx", "tp"), P(None, None, "tp"), P("ctx", "tp"), P("tp"), P("tp", None))
    return jax.shard_map(body, mesh=mesh, in_specs=placed, out_specs=P("ctx", "tp"), check_vma=False)
```

```python
import functools

import jax
import jax.numpy as jnp
import numpy as np
from jax import lax
from jax.experimental import pallas as pl
from jax.experimental.pallas import tpu as pltpu
from jax.sharding import PartitionSpec as P

MESH = pl.DeviceIdType.MESH
GROUP = 13
LANE = 128
HALO = 16


def tables(blocks, width, lanes):
    freqs = blocks + 1
    points = 2 * blocks * width
    f = np.arange(freqs)
    angle = 2.0 * np.pi * np.outer(f, np.arange(blocks)) / (2 * blocks)
    steps = freqs // GROUP
    eye = np.eye(lanes)
    pair = np.stack([np.cos(angle), -np.sin(angle)]).reshape(2, steps, GROUP, blocks)
    pair = pair.transpose(1, 0, 2, 3).reshape(2 * freqs, blocks)
    lead = np.kron(pair, eye)
    weight = np.where((f == 0) | (f == blocks), 1.0, 2.0)[:, None] / points
    turn = 2.0 * np.pi * np.outer(f, np.arange(width)) / points
    twiddle = np.stack([np.cos(turn), -np.sin(turn)])
    twiddle = np.repeat(twiddle, lanes, axis=1)
    inner = 2.0 * np.pi * np.outer(np.arange(width), np.arange(width)) / width
    c, s = np.cos(inner), np.sin(inner)
    forward = np.block([[c, -s], [s, c]])
    backward = np.block([[c, s], [-s, c]])
    scaled = np.stack([np.cos(angle) * weight, -np.sin(angle) * weight]).reshape(2, steps, GROUP, blocks)
    scaled = scaled.transpose(1, 0, 2, 3).reshape(2 * freqs, blocks)
    tail = np.kron(scaled.T, eye)
    half = jnp.bfloat16
    return (
        lead.astype(half),
        tail.astype(half),
        twiddle.astype(np.float32),
        forward.astype(half),
        backward.astype(half),
    )


def dot(left, right):
    return jnp.dot(left, right, preferred_element_type=jnp.float32)


def kernel(
    blocks,
    tps,
    lanes,
    qkv_hbm,
    taps_ref,
    filter_hbm,
    skip_ref,
    weight_hbm,
    lead_hbm,
    tail_hbm,
    twiddle_hbm,
    forward_hbm,
    backward_hbm,
    out_ref,
    qkv_ref,
    filter_ref,
    weight_ref,
    lead_ref,
    tail_ref,
    twiddle_ref,
    forward_ref,
    backward_ref,
    halo_ref,
    filter_t,
    signal_t,
    signal_ref,
    query_ref,
    h_ref,
    x_ref,
    sh_ref,
    back_ref,
    y_ref,
    conv_ref,
    gated_ref,
    relay_src,
    relay_in,
    part_ref,
    send_ref,
    take_ref,
    load_sem,
    halo_sem,
    filter_sem,
    signal_sem,
    conv_send,
    conv_recv,
    tp_send,
    tp_recv,
):
    f32 = jnp.float32
    bf16 = jnp.bfloat16
    me = lax.axis_index("ctx")
    col = lax.axis_index("tp")
    tokens, channels = filter_ref.shape
    half_tok = tokens // 2
    half_col = out_ref.shape[1] // 2
    cols = out_ref.shape[1]

    sources = (filter_hbm, qkv_hbm, lead_hbm, twiddle_hbm, forward_hbm, weight_hbm, backward_hbm, tail_hbm)
    targets = (filter_ref, qkv_ref, lead_ref, twiddle_ref, forward_ref, weight_ref, backward_ref, tail_ref)
    loads = [pltpu.make_async_copy(s, t, load_sem.at[i]) for i, (s, t) in enumerate(zip(sources, targets))]
    for load in loads:
        load.start()

    barrier = pltpu.get_barrier_semaphore()

    def greet(i, carry):
        pl.semaphore_signal(barrier, inc=1, device_id={"ctx": lax.rem(me + i, blocks)}, device_id_type=MESH)
        return carry

    lax.fori_loop(1, blocks, greet, 0)
    right = lax.rem(col + 1, tps)
    left = lax.rem(col + tps - 1, tps)
    for side in (left, right):
        pl.semaphore_signal(barrier, inc=1, device_id={"tp": side}, device_id_type=MESH)

    per = LANE // lanes
    chunks = channels // LANE

    def piece(ref, p):
        return ref.at[pl.ds(pl.multiple_of(p * lanes, lanes), lanes)]

    def chunk_at(i):
        return pl.ds(pl.multiple_of(i * LANE, LANE), LANE)

    def scatter(src, dst, sems, chunk):
        def one(k, carry):
            p = chunk * per + lax.rem(me + k, per)

            @pl.when(p != me)
            def _():
                pltpu.make_async_remote_copy(
                    piece(src, p), piece(dst, me), sems.at[0], sems.at[1], device_id={"ctx": p}, device_id_type=MESH
                ).start()

            return carry

        lax.fori_loop(0, per, one, 0)

    def settled(src, dst, sems):
        rows = (blocks - 1) * lanes
        return pltpu.make_async_remote_copy(
            src.at[pl.ds(0, rows)],
            dst.at[pl.ds(0, rows)],
            sems.at[0],
            sems.at[1],
            device_id={"ctx": me},
            device_id_type=MESH,
        )

    own = pl.ds(pl.multiple_of(me * lanes, lanes), lanes)

    loads[0].wait()

    def flip(i, carry):
        at = chunk_at(i)
        filter_t[at, :] = filter_ref[:, at].astype(f32).T.astype(bf16)
        return carry

    lax.fori_loop(0, chunks, flip, 0)
    loads[1].wait()
    pl.semaphore_wait(barrier, blocks + 1)

    halo = pltpu.make_async_remote_copy(
        qkv_ref.at[:, pl.ds(tokens - HALO, HALO)],
        halo_ref,
        halo_sem.at[0],
        halo_sem.at[1],
        device_id={"ctx": lax.rem(me + 1, blocks)},
        device_id_type=MESH,
    )
    halo.start()

    def send_filter(i, carry):
        scatter(filter_t, h_ref, filter_sem, lax.rem(me // per + i, chunks))
        return carry

    lax.fori_loop(0, chunks, send_filter, 0)
    h_ref[own, :] = filter_t[own, :]
    halo.wait()

    def shortened(i, at):
        edge = jnp.where(me > 0, halo_ref[i, :, at].astype(f32), 0.0)
        wide = jnp.concatenate([edge, qkv_ref[i, :, at].astype(f32)], axis=0)
        return (
            taps_ref[i, 0:1, at] * wide[HALO:]
            + taps_ref[i, 1:2, at] * wide[HALO - 1 : HALO - 1 + tokens]
            + taps_ref[i, 2:3, at] * wide[HALO - 2 : HALO - 2 + tokens]
        )

    def send_signal(i, carry):
        chunk = lax.rem(me // per + i, chunks)
        at = chunk_at(chunk)
        signal = (shortened(1, at) * shortened(2, at)).astype(bf16)
        signal_ref[:, at] = signal
        signal_t[at, :] = signal.astype(f32).T.astype(bf16)
        scatter(signal_t, x_ref, signal_sem, chunk)
        return carry

    lax.fori_loop(0, chunks, send_signal, 0)
    x_ref[own, :] = signal_t[own, :]

    def query(i, carry):
        at = chunk_at(i)
        query_ref[:, at] = shortened(0, at)
        return carry

    lax.fori_loop(0, chunks, query, 0)

    width = tokens
    rows = GROUP * lanes
    steps = (blocks + 1) // GROUP

    def tables_at(i):
        at = pl.ds(pl.multiple_of(i * rows, 16), rows)
        at2 = pl.ds(pl.multiple_of(i * 2 * rows, 16), 2 * rows)
        return at, at2, twiddle_ref[0, at, :], twiddle_ref[1, at, :]

    def spectrum(ref, i):
        _, at2, cos, sin = tables_at(i)
        first = dot(lead_ref[at2, :], ref[...])
        real, imag = first[:rows], first[rows:]
        turned = jnp.concatenate([real * cos - imag * sin, real * sin + imag * cos], axis=1)
        return dot(turned.astype(bf16), forward_ref[...])

    for load in loads[2:5]:
        load.wait()
    from_filter = settled(filter_t, h_ref, filter_sem)
    from_filter.wait_recv()

    def filter_step(i, carry):
        at = tables_at(i)[0]
        sh_ref[at, :] = spectrum(h_ref, i).astype(bf16)
        return carry

    lax.fori_loop(0, steps, filter_step, 0)
    for load in loads[5:]:
        load.wait()
    from_filter.wait_send()
    from_signal = settled(signal_t, x_ref, signal_sem)
    from_signal.wait_recv()

    def signal_step(i, carry):
        at, at2, cos, sin = tables_at(i)
        sx = spectrum(x_ref, i)
        xr, xi = sx[:, :width], sx[:, width:]
        hr, hi = sh_ref[at, :width].astype(f32), sh_ref[at, width:].astype(f32)
        product = jnp.concatenate([xr * hr - xi * hi, xr * hi + xi * hr], axis=1)
        back = dot(product.astype(bf16), backward_ref[...])
        br, bi = back[:, :width], back[:, width:]
        out = jnp.concatenate([br * cos + bi * sin, bi * cos - br * sin], axis=0)
        back_ref[at2, :] = out.astype(bf16)
        return carry

    lax.fori_loop(0, steps, signal_step, 0)

    group = 16
    big = group * lanes
    turns = blocks // group

    def send_conv(i, h):
        first = lax.rem(me // group + i, turns) * group

        def one(k, carry):
            p = first + lax.rem(me + k, group)

            @pl.when(p != me)
            def _():
                pltpu.make_async_remote_copy(
                    piece(y_ref.at[h], p),
                    piece(conv_ref.at[h], me),
                    conv_send.at[h],
                    conv_recv.at[h],
                    device_id={"ctx": p},
                    device_id_type=MESH,
                ).start()

            return carry

        lax.fori_loop(0, group, one, 0)

    def last_step(i, carry):
        at = pl.ds(pl.multiple_of(lax.rem(me // group + i, turns) * big, 16), big)
        y = dot(tail_ref[at, :], back_ref[...]).astype(bf16)
        y_ref[0, at, :] = y[:, :half_tok]
        y_ref[1, at, :] = y[:, half_tok:]
        send_conv(i, 0)
        return carry

    lax.fori_loop(0, turns, last_step, 0)

    def rest_step(i, carry):
        send_conv(i, 1)
        return carry

    lax.fori_loop(0, turns, rest_step, 0)
    from_conv = []
    for h in range(2):
        conv_ref[h, own, :] = y_ref[h, own, :]
        rows_all = pl.ds(0, (blocks - 1) * lanes)
        from_conv.append(
            pltpu.make_async_remote_copy(
                y_ref.at[h, rows_all],
                conv_ref.at[h, rows_all],
                conv_send.at[h],
                conv_recv.at[h],
                device_id={"ctx": me},
                device_id_type=MESH,
            )
        )

    def tp_copy(src, dst, h, kind, side):
        s = (h * 3 + kind) * 2 + side
        return pltpu.make_async_remote_copy(
            src, dst, tp_send.at[s], tp_recv.at[s], device_id={"tp": (right, left)[side]}, device_id_type=MESH
        )

    def product(h, dest, start):
        at = pl.ds(pl.multiple_of(dest * cols + start, half_col), half_col)
        return dot(gated_ref[h], weight_ref[:, at])

    far = lax.rem(col + 2, tps)
    relays, opens, sums = [], [], []
    for h in range(2):
        from_conv[h].wait_recv()
        tok = pl.ds(h * half_tok, half_tok)

        def gate(i, carry):
            at = chunk_at(i)
            conv = conv_ref[h, at, :].astype(f32).T
            signal = signal_ref[tok, at].astype(f32)
            gated_ref[h, :, at] = (query_ref[tok, at] * (conv + skip_ref[:, at] * signal)).astype(bf16)
            return carry

        lax.fori_loop(0, chunks, gate, 0)
        for side in range(2):
            relay_src[h, side] = product(h, far, side * half_col).astype(bf16)
            copy = tp_copy(relay_src.at[h, side], relay_in.at[h, side], h, 0, side)
            copy.start()
            relays.append(copy)
        for side, dest in ((0, right), (1, left)):
            send_ref[h, side, 1] = product(h, dest, (1 - side) * half_col).astype(bf16)
            copy = tp_copy(send_ref.at[h, side, 1], take_ref.at[h, side, 1], h, 1, side)
            copy.start()
            opens.append(copy)
        for side, dest in ((0, right), (1, left)):
            part_ref[side] = product(h, dest, side * half_col)
        for side in range(2):
            relays[2 * h + side].wait_recv()
            send_ref[h, side, 0] = (part_ref[side] + relay_in[h, side].astype(f32)).astype(bf16)
            copy = tp_copy(send_ref.at[h, side, 0], take_ref.at[h, side, 0], h, 2, side)
            copy.start()
            sums.append(copy)
        for part in range(2):
            part_ref[2 + 2 * h + part] = product(h, col, part * half_col)

    for h in range(2):
        for side in range(2):
            opens[2 * h + side].wait_recv()
            sums[2 * h + side].wait_recv()
        tok = pl.ds(h * half_tok, half_tok)
        for part in range(2):
            total = (
                part_ref[2 + 2 * h + part]
                + take_ref[h, 0, part].astype(f32)
                + take_ref[h, 1, 1 - part].astype(f32)
            )
            out_ref[tok, pl.ds(part * half_col, half_col)] = total.astype(bf16)

    from_signal.wait_send()
    for copy in from_conv + relays + opens + sums:
        copy.wait_send()


def body(qkv, short_taps, long_filter, skip, out_weight):
    blocks = lax.axis_size("ctx")
    tps = lax.axis_size("tp")
    tokens, channels = qkv.shape[1:]
    lanes = channels // blocks
    cols = out_weight.shape[1] // tps
    consts = [jnp.asarray(c) for c in tables(blocks, tokens, lanes)]
    freqs = (blocks + 1) * lanes
    vmem = pl.BlockSpec(memory_space=pltpu.VMEM)
    hbm = pl.BlockSpec(memory_space=pl.ANY)
    bf16 = jnp.bfloat16
    f32 = jnp.float32
    dma = pltpu.SemaphoreType.DMA
    half = tokens // 2
    return pl.pallas_call(
        functools.partial(kernel, blocks, tps, lanes),
        out_shape=jax.ShapeDtypeStruct((tokens, cols), bf16),
        in_specs=[hbm, vmem, hbm, vmem] + [hbm] * 6,
        out_specs=vmem,
        scratch_shapes=[
            pltpu.VMEM(qkv.shape, bf16),
            pltpu.VMEM((tokens, channels), bf16),
            pltpu.VMEM(out_weight.shape, bf16),
            *[pltpu.VMEM(c.shape, c.dtype) for c in consts],
            pltpu.VMEM((3, HALO, channels), bf16),
            pltpu.VMEM((channels, tokens), bf16),
            pltpu.VMEM((channels, tokens), bf16),
            pltpu.VMEM((tokens, channels), bf16),
            pltpu.VMEM((tokens, channels), f32),
            pltpu.VMEM((channels, tokens), bf16),
            pltpu.VMEM((channels, tokens), bf16),
            pltpu.VMEM((freqs, 2 * tokens), bf16),
            pltpu.VMEM((2 * freqs, tokens), bf16),
            pltpu.VMEM((2, channels, half), bf16),
            pltpu.VMEM((2, channels, half), bf16),
            pltpu.VMEM((2, half, channels), bf16),
            pltpu.VMEM((2, 2, half, cols // 2), bf16),
            pltpu.VMEM((2, 2, half, cols // 2), bf16),
            pltpu.VMEM((6, half, cols // 2), f32),
            pltpu.VMEM((2, 2, 2, half, cols // 2), bf16),
            pltpu.VMEM((2, 2, 2, half, cols // 2), bf16),
            dma((8,)),
            dma((2,)),
            dma((2,)),
            dma((2,)),
            dma((2,)),
            dma((2,)),
            dma((12,)),
            dma((12,)),
        ],
        compiler_params=pltpu.CompilerParams(
            collective_id=0, has_side_effects=True, vmem_limit_bytes=56 << 20
        ),
        name="hyena",
    )(qkv, short_taps, long_filter, skip[None, :], out_weight, *consts)


def solution(mesh):
    placed = (P(None, "ctx", "tp"), P(None, None, "tp"), P("ctx", "tp"), P("tp"), P("tp", None))
    return jax.shard_map(body, mesh=mesh, in_specs=placed, out_specs=P("ctx", "tp"), check_vma=False)
```

```python
import functools

import jax
import jax.numpy as jnp
import numpy as np
from jax import lax
from jax.experimental import pallas as pl
from jax.experimental.pallas import tpu as pltpu
from jax.sharding import PartitionSpec as P

MESH = pl.DeviceIdType.MESH
LANE = 128
HALO = 16


def tables(blocks, width, lanes):
    f = np.arange(blocks)
    points = 2 * blocks * width
    angle = 2.0 * np.pi * np.outer(f, np.arange(blocks)) / (2 * blocks)
    real, imag = np.cos(angle), -np.sin(angle)
    imag[0] = np.cos(np.pi * f)
    weight = np.where(f == 0, 1.0, 2.0)[:, None] / points
    back_real, back_imag = real * weight, imag * weight
    back_imag[0] = imag[0] / points
    turn = 2.0 * np.pi * np.outer(np.minimum(np.arange(blocks + lanes), blocks), np.arange(width)) / points
    inner = 2.0 * np.pi * np.outer(np.arange(width), np.arange(width)) / width
    c, s = np.cos(inner), np.sin(inner)
    half = jnp.bfloat16
    return (
        np.concatenate([real, imag]).astype(half),
        np.concatenate([back_real, back_imag]).T.astype(half),
        np.stack([np.cos(turn), -np.sin(turn)]).astype(np.float32),
        np.block([[c, -s], [s, c]]).astype(half),
        np.block([[c, s], [-s, c]]).astype(half),
    )


def dot(left, right):
    return jnp.dot(left, right, preferred_element_type=jnp.float32)


def kernel(
    blocks,
    tps,
    lanes,
    qkv_hbm,
    taps_ref,
    filter_hbm,
    skip_ref,
    weight_hbm,
    lead_hbm,
    tail_hbm,
    twiddle_hbm,
    forward_hbm,
    backward_hbm,
    out_ref,
    qkv_ref,
    filter_ref,
    weight_ref,
    lead_ref,
    tail_ref,
    twiddle_ref,
    forward_ref,
    backward_ref,
    halo_ref,
    filter_t,
    signal_t,
    signal_ref,
    query_ref,
    h_ref,
    x_ref,
    sh_ref,
    wide_ref,
    y_ref,
    conv_ref,
    gated_ref,
    relay_src,
    relay_in,
    part_ref,
    send_ref,
    take_ref,
    load_sem,
    halo_sem,
    filter_sem,
    signal_sem,
    conv_send,
    conv_recv,
    tp_send,
    tp_recv,
):
    f32 = jnp.float32
    bf16 = jnp.bfloat16
    me = lax.axis_index("ctx")
    col = lax.axis_index("tp")
    tokens, channels = filter_ref.shape
    half_tok = tokens // 2
    half_col = out_ref.shape[1] // 2
    cols = out_ref.shape[1]

    sources = (filter_hbm, qkv_hbm, lead_hbm, twiddle_hbm, forward_hbm, weight_hbm, backward_hbm, tail_hbm)
    targets = (filter_ref, qkv_ref, lead_ref, twiddle_ref, forward_ref, weight_ref, backward_ref, tail_ref)
    loads = [pltpu.make_async_copy(s, t, load_sem.at[i]) for i, (s, t) in enumerate(zip(sources, targets))]
    for load in loads:
        load.start()

    barrier = pltpu.get_barrier_semaphore()

    def greet(i, carry):
        pl.semaphore_signal(barrier, inc=1, device_id={"ctx": lax.rem(me + i, blocks)}, device_id_type=MESH)
        return carry

    lax.fori_loop(1, blocks, greet, 0)
    right = lax.rem(col + 1, tps)
    left = lax.rem(col + tps - 1, tps)
    for side in (left, right):
        pl.semaphore_signal(barrier, inc=1, device_id={"tp": side}, device_id_type=MESH)

    per = LANE // lanes
    chunks = channels // LANE

    def piece(ref, p):
        return ref.at[pl.ds(pl.multiple_of(p * lanes, lanes), lanes)]

    def chunk_at(i):
        return pl.ds(pl.multiple_of(i * LANE, LANE), LANE)

    def scatter(src, dst, sems, chunk):
        def one(k, carry):
            p = chunk * per + lax.rem(me + k, per)

            @pl.when(p != me)
            def _():
                pltpu.make_async_remote_copy(
                    piece(src, p), piece(dst, me), sems.at[0], sems.at[1], device_id={"ctx": p}, device_id_type=MESH
                ).start()

            return carry

        lax.fori_loop(0, per, one, 0)

    def settled(src, dst, sems):
        rows = (blocks - 1) * lanes
        return pltpu.make_async_remote_copy(
            src.at[pl.ds(0, rows)],
            dst.at[pl.ds(0, rows)],
            sems.at[0],
            sems.at[1],
            device_id={"ctx": me},
            device_id_type=MESH,
        )

    own = pl.ds(pl.multiple_of(me * lanes, lanes), lanes)

    loads[0].wait()

    def flip(i, carry):
        at = chunk_at(i)
        filter_t[at, :] = filter_ref[:, at].astype(f32).T.astype(bf16)
        return carry

    lax.fori_loop(0, chunks, flip, 0)
    loads[1].wait()
    pl.semaphore_wait(barrier, blocks + 1)

    halo = pltpu.make_async_remote_copy(
        qkv_ref.at[:, pl.ds(tokens - HALO, HALO)],
        halo_ref,
        halo_sem.at[0],
        halo_sem.at[1],
        device_id={"ctx": lax.rem(me + 1, blocks)},
        device_id_type=MESH,
    )
    halo.start()

    def send_filter(i, carry):
        scatter(filter_t, h_ref, filter_sem, lax.rem(me // per + i, chunks))
        return carry

    lax.fori_loop(0, chunks, send_filter, 0)
    h_ref[own, :] = filter_t[own, :]
    halo.wait()

    def shortened(i, at):
        edge = jnp.where(me > 0, halo_ref[i, :, at].astype(f32), 0.0)
        wide = jnp.concatenate([edge, qkv_ref[i, :, at].astype(f32)], axis=0)
        return (
            taps_ref[i, 0:1, at] * wide[HALO:]
            + taps_ref[i, 1:2, at] * wide[HALO - 1 : HALO - 1 + tokens]
            + taps_ref[i, 2:3, at] * wide[HALO - 2 : HALO - 2 + tokens]
        )

    def send_signal(i, carry):
        chunk = lax.rem(me // per + i, chunks)
        at = chunk_at(chunk)
        signal = (shortened(1, at) * shortened(2, at)).astype(bf16)
        signal_ref[:, at] = signal
        signal_t[at, :] = signal.astype(f32).T.astype(bf16)
        scatter(signal_t, x_ref, signal_sem, chunk)
        return carry

    lax.fori_loop(0, chunks, send_signal, 0)
    x_ref[own, :] = signal_t[own, :]

    def query(i, carry):
        at = chunk_at(i)
        query_ref[:, at] = shortened(0, at)
        return carry

    lax.fori_loop(0, chunks, query, 0)

    width = tokens
    first_row = lax.broadcasted_iota(jnp.int32, (blocks, width), 0) == 0
    halves = (slice(0, half_tok), slice(half_tok, tokens))

    def turns_of():
        return twiddle_ref[0, :blocks], twiddle_ref[1, :blocks], twiddle_ref[0, blocks:], twiddle_ref[1, blocks:]

    def spectrum(ref):
        cos, sin, cos_last, sin_last = turns_of()
        for h, part in enumerate(halves):
            wide_ref[h] = ref[:, part].astype(f32)
        turned, last = [], []
        for c in range(lanes):
            picked = pl.ds(c, blocks, stride=lanes)
            column = jnp.concatenate([wide_ref[0, picked, :], wide_ref[1, picked, :]], axis=1).astype(bf16)
            first = dot(lead_ref[...], column)
            real, imag = first[:blocks], first[blocks:]
            last.append(imag[0:1])
            imag = jnp.where(first_row, 0.0, imag)
            turned.append(jnp.concatenate([real * cos - imag * sin, real * sin + imag * cos], axis=1).astype(bf16))
        last = jnp.concatenate(last, axis=0)
        turned.append(jnp.concatenate([last * cos_last, last * sin_last], axis=1).astype(bf16))
        return dot(jnp.concatenate(turned, axis=0), forward_ref[...])

    for load in loads[2:5]:
        load.wait()
    from_filter = settled(filter_t, h_ref, filter_sem)
    from_filter.wait_recv()

    sh_ref[...] = spectrum(h_ref).astype(bf16)
    for load in loads[5:]:
        load.wait()
    from_filter.wait_send()
    from_signal = settled(signal_t, x_ref, signal_sem)
    from_signal.wait_recv()

    sx = spectrum(x_ref)
    xr, xi = sx[:, :width], sx[:, width:]
    hr, hi = sh_ref[:, :width].astype(f32), sh_ref[:, width:].astype(f32)
    product = jnp.concatenate([xr * hr - xi * hi, xr * hi + xi * hr], axis=1).astype(bf16)
    back = dot(product, backward_ref[...])
    br, bi = back[:, :width], back[:, width:]
    cos, sin, cos_last, sin_last = turns_of()
    last = br[lanes * blocks :] * cos_last + bi[lanes * blocks :] * sin_last
    for c in range(lanes):
        at = slice(c * blocks, (c + 1) * blocks)
        real, imag = br[at], bi[at]
        imag_turned = jnp.where(first_row, last[c : c + 1], imag * cos - real * sin)
        turned = jnp.concatenate([real * cos + imag * sin, imag_turned], axis=0).astype(bf16)
        y = dot(tail_ref[...], turned)
        for h, part in enumerate(halves):
            wide_ref[h, pl.ds(c, blocks, stride=lanes), :] = y[:, part]

    def send_conv(h):
        def one(i, carry):
            p = lax.rem(me + i, blocks)
            pltpu.make_async_remote_copy(
                piece(y_ref.at[h], p),
                piece(conv_ref.at[h], me),
                conv_send.at[h],
                conv_recv.at[h],
                device_id={"ctx": p},
                device_id_type=MESH,
            ).start()
            return carry

        lax.fori_loop(1, blocks, one, 0)

    for h in range(2):
        y_ref[h] = wide_ref[h].astype(bf16)
        send_conv(h)
    from_conv = []
    for h in range(2):
        conv_ref[h, own, :] = y_ref[h, own, :]
        rows_all = pl.ds(0, (blocks - 1) * lanes)
        from_conv.append(
            pltpu.make_async_remote_copy(
                y_ref.at[h, rows_all],
                conv_ref.at[h, rows_all],
                conv_send.at[h],
                conv_recv.at[h],
                device_id={"ctx": me},
                device_id_type=MESH,
            )
        )

    def tp_copy(src, dst, h, kind, side):
        s = (h * 3 + kind) * 2 + side
        return pltpu.make_async_remote_copy(
            src, dst, tp_send.at[s], tp_recv.at[s], device_id={"tp": (right, left)[side]}, device_id_type=MESH
        )

    def project(h, dest, start):
        at = pl.ds(pl.multiple_of(dest * cols + start, half_col), half_col)
        return dot(gated_ref[h], weight_ref[:, at])

    far = lax.rem(col + 2, tps)
    relays, opens, sums = [], [], []
    for h in range(2):
        from_conv[h].wait_recv()
        tok = pl.ds(h * half_tok, half_tok)

        for i in range(chunks):
            at = slice(i * LANE, (i + 1) * LANE)
            conv = conv_ref[h, at, :].astype(f32).T
            signal = signal_ref[tok, at].astype(f32)
            gated_ref[h, :, at] = (query_ref[tok, at] * (conv + skip_ref[:, at] * signal)).astype(bf16)
        for side in range(2):
            relay_src[h, side] = project(h, far, side * half_col).astype(bf16)
            copy = tp_copy(relay_src.at[h, side], relay_in.at[h, side], h, 0, side)
            copy.start()
            relays.append(copy)
        for side, dest in ((0, right), (1, left)):
            send_ref[h, side, 1] = project(h, dest, (1 - side) * half_col).astype(bf16)
            copy = tp_copy(send_ref.at[h, side, 1], take_ref.at[h, side, 1], h, 1, side)
            copy.start()
            opens.append(copy)
        for side, dest in ((0, right), (1, left)):
            part_ref[side] = project(h, dest, side * half_col)
        for side in range(2):
            relays[2 * h + side].wait_recv()
            send_ref[h, side, 0] = (part_ref[side] + relay_in[h, side].astype(f32)).astype(bf16)
            copy = tp_copy(send_ref.at[h, side, 0], take_ref.at[h, side, 0], h, 2, side)
            copy.start()
            sums.append(copy)
        for part in range(2):
            part_ref[2 + 2 * h + part] = project(h, col, part * half_col)

    for h in range(2):
        for side in range(2):
            opens[2 * h + side].wait_recv()
            sums[2 * h + side].wait_recv()
        tok = pl.ds(h * half_tok, half_tok)
        for part in range(2):
            total = (
                part_ref[2 + 2 * h + part]
                + take_ref[h, 0, part].astype(f32)
                + take_ref[h, 1, 1 - part].astype(f32)
            )
            out_ref[tok, pl.ds(part * half_col, half_col)] = total.astype(bf16)

    from_signal.wait_send()
    for copy in from_conv + relays + opens + sums:
        copy.wait_send()


def body(qkv, short_taps, long_filter, skip, out_weight):
    blocks = lax.axis_size("ctx")
    tps = lax.axis_size("tp")
    tokens, channels = qkv.shape[1:]
    lanes = channels // blocks
    cols = out_weight.shape[1] // tps
    consts = [jnp.asarray(c) for c in tables(blocks, tokens, lanes)]
    freqs = (blocks + 1) * lanes
    vmem = pl.BlockSpec(memory_space=pltpu.VMEM)
    hbm = pl.BlockSpec(memory_space=pl.ANY)
    bf16 = jnp.bfloat16
    f32 = jnp.float32
    dma = pltpu.SemaphoreType.DMA
    half = tokens // 2
    return pl.pallas_call(
        functools.partial(kernel, blocks, tps, lanes),
        out_shape=jax.ShapeDtypeStruct((tokens, cols), bf16),
        in_specs=[hbm, vmem, hbm, vmem] + [hbm] * 6,
        out_specs=vmem,
        scratch_shapes=[
            pltpu.VMEM(qkv.shape, bf16),
            pltpu.VMEM((tokens, channels), bf16),
            pltpu.VMEM(out_weight.shape, bf16),
            *[pltpu.VMEM(c.shape, c.dtype) for c in consts],
            pltpu.VMEM((3, HALO, channels), bf16),
            pltpu.VMEM((channels, tokens), bf16),
            pltpu.VMEM((channels, tokens), bf16),
            pltpu.VMEM((tokens, channels), bf16),
            pltpu.VMEM((tokens, channels), f32),
            pltpu.VMEM((channels, tokens), bf16),
            pltpu.VMEM((channels, tokens), bf16),
            pltpu.VMEM((freqs, 2 * tokens), bf16),
            pltpu.VMEM((2, channels, half), f32),
            pltpu.VMEM((2, channels, half), bf16),
            pltpu.VMEM((2, channels, half), bf16),
            pltpu.VMEM((2, half, channels), bf16),
            pltpu.VMEM((2, 2, half, cols // 2), bf16),
            pltpu.VMEM((2, 2, half, cols // 2), bf16),
            pltpu.VMEM((6, half, cols // 2), f32),
            pltpu.VMEM((2, 2, 2, half, cols // 2), bf16),
            pltpu.VMEM((2, 2, 2, half, cols // 2), bf16),
            dma((8,)),
            dma((2,)),
            dma((2,)),
            dma((2,)),
            dma((2,)),
            dma((2,)),
            dma((12,)),
            dma((12,)),
        ],
        compiler_params=pltpu.CompilerParams(
            collective_id=0, has_side_effects=True, vmem_limit_bytes=56 << 20
        ),
        name="hyena",
    )(qkv, short_taps, long_filter, skip[None, :], out_weight, *consts)


def solution(mesh):
    placed = (P(None, "ctx", "tp"), P(None, None, "tp"), P("ctx", "tp"), P("tp"), P("tp", None))
    return jax.shard_map(body, mesh=mesh, in_specs=placed, out_specs=P("ctx", "tp"), check_vma=False)
```

```python
import functools

import jax
import jax.numpy as jnp
import numpy as np
from jax import lax
from jax.experimental import pallas as pl
from jax.experimental.pallas import tpu as pltpu
from jax.sharding import PartitionSpec as P

MESH = pl.DeviceIdType.MESH
LANE = 128
LINE = 16
HALO = 16


def tables(blocks, width, lanes):
    f = np.arange(blocks)
    points = 2 * blocks * width
    angle = 2.0 * np.pi * np.outer(f, np.arange(blocks)) / (2 * blocks)
    real, imag = np.cos(angle), -np.sin(angle)
    imag[0] = np.cos(np.pi * f)
    weight = np.where(f == 0, 1.0, 2.0)[:, None] / points
    back_real, back_imag = real * weight, imag * weight
    back_imag[0] = imag[0] / points
    turn = 2.0 * np.pi * np.outer(np.minimum(np.arange(blocks + lanes), blocks), np.arange(width)) / points
    inner = 2.0 * np.pi * np.outer(np.arange(width), np.arange(width)) / width
    c, s = np.cos(inner), np.sin(inner)
    half = jnp.bfloat16
    return (
        np.concatenate([real, imag]).astype(half),
        np.concatenate([back_real, back_imag]).T.astype(half),
        np.stack([np.cos(turn), -np.sin(turn)]).astype(np.float32),
        np.block([[c, -s], [s, c]]).astype(half),
        np.block([[c, s], [-s, c]]).astype(half),
    )


def dot(left, right):
    return jnp.dot(left, right, preferred_element_type=jnp.float32)


def kernel(
    blocks,
    tps,
    lanes,
    qkv_hbm,
    taps_ref,
    filter_hbm,
    skip_ref,
    weight_hbm,
    lead_hbm,
    tail_hbm,
    twiddle_hbm,
    forward_hbm,
    backward_hbm,
    out_ref,
    qkv_ref,
    filter_ref,
    weight_ref,
    lead_ref,
    tail_ref,
    twiddle_ref,
    forward_ref,
    backward_ref,
    halo_ref,
    filter_t,
    signal_t,
    filter_line,
    signal_strip,
    signal_ref,
    query_ref,
    h_ref,
    x_ref,
    sh_ref,
    wide_ref,
    y_ref,
    conv_ref,
    gated_ref,
    relay_src,
    relay_in,
    part_ref,
    send_ref,
    take_ref,
    load_sem,
    halo_sem,
    filter_send,
    filter_recv,
    signal_hop,
    filter_sem,
    signal_sem,
    conv_send,
    conv_recv,
    tp_send,
    tp_recv,
):
    f32 = jnp.float32
    bf16 = jnp.bfloat16
    me = lax.axis_index("ctx")
    col = lax.axis_index("tp")
    tokens, channels = filter_ref.shape
    half_tok = tokens // 2
    half_col = out_ref.shape[1] // 2
    cols = out_ref.shape[1]

    sources = (filter_hbm, qkv_hbm, lead_hbm, twiddle_hbm, forward_hbm, weight_hbm, backward_hbm, tail_hbm)
    targets = (filter_ref, qkv_ref, lead_ref, twiddle_ref, forward_ref, weight_ref, backward_ref, tail_ref)
    loads = [pltpu.make_async_copy(s, t, load_sem.at[i]) for i, (s, t) in enumerate(zip(sources, targets))]
    for load in loads:
        load.start()

    barrier = pltpu.get_barrier_semaphore()

    ys = blocks // LINE
    y = me // LINE
    spot = lax.rem(me, LINE)
    strip_rows = LINE * lanes

    def greet(i, carry):
        peer = y * LINE + lax.rem(spot + i, LINE)
        pl.semaphore_signal(barrier, inc=1, device_id={"ctx": peer}, device_id_type=MESH)
        return carry

    lax.fori_loop(1, LINE, greet, 0)
    for back_by in [LINE * dy for dy in range(1, ys)] + [1]:
        peer = lax.rem(me + blocks - back_by, blocks)
        pl.semaphore_signal(barrier, inc=1, device_id={"ctx": peer}, device_id_type=MESH)
    right = lax.rem(col + 1, tps)
    left = lax.rem(col + tps - 1, tps)
    for side in (left, right):
        pl.semaphore_signal(barrier, inc=1, device_id={"tp": side}, device_id_type=MESH)

    chunks = channels // LANE

    def piece(ref, p):
        return ref.at[pl.ds(pl.multiple_of(p * lanes, lanes), lanes)]

    def chunk_at(i):
        return pl.ds(pl.multiple_of(i * LANE, LANE), LANE)

    def rows_of(block, count):
        return pl.ds(pl.multiple_of(block * lanes, lanes), count * lanes)

    def cross(src, strip, sems, dy):
        to = lax.rem(y + dy, ys)
        return pltpu.make_async_remote_copy(
            src.at[rows_of(to * LINE, LINE)],
            strip.at[dy - 1],
            sems.at[0, dy - 1],
            sems.at[1, dy - 1],
            device_id={"ctx": to * LINE + spot},
            device_id_type=MESH,
        )

    def along(src, first, dst, dst_sems, origin):
        there = rows_of(origin * LINE + spot, 1)

        def one(i, carry):
            peer = lax.rem(spot + i, LINE)
            pltpu.make_async_remote_copy(
                src.at[rows_of(first + peer, 1)],
                dst.at[there],
                dst_sems.at[0],
                dst_sems.at[1],
                device_id={"ctx": y * LINE + peer},
                device_id_type=MESH,
            ).start()
            return carry

        lax.fori_loop(1, LINE, one, 0)
        dst[there, :] = src[rows_of(first + spot, 1), :]

    def settled(src, dst, sems, pieces):
        rows = pieces * lanes
        return pltpu.make_async_remote_copy(
            src.at[pl.ds(0, rows)],
            dst.at[pl.ds(0, rows)],
            sems.at[0],
            sems.at[1],
            device_id={"ctx": me},
            device_id_type=MESH,
        )

    own = rows_of(me, 1)
    nearest = sorted(range(1, ys), key=lambda dy: min(dy, ys - dy))

    loads[0].wait()

    per = LANE // lanes
    for i in range(chunks):
        turned = filter_ref[:, i * LANE : (i + 1) * LANE].astype(f32).T.astype(bf16)
        place = slice(i * per % LINE, i * per % LINE + per)
        filter_t[i * per // LINE, place] = turned.reshape(per, lanes, tokens)
    loads[1].wait()
    pl.semaphore_wait(barrier, LINE + ys + 1)

    halo = pltpu.make_async_remote_copy(
        qkv_ref.at[:, pl.ds(tokens - HALO, HALO)],
        halo_ref,
        halo_sem.at[0],
        halo_sem.at[1],
        device_id={"ctx": lax.rem(me + 1, blocks)},
        device_id_type=MESH,
    )
    halo.start()

    def along_filter(i, carry):
        peer = lax.rem(spot + i, LINE)
        pltpu.make_async_remote_copy(
            filter_t.at[:, peer],
            filter_line.at[i],
            filter_send.at[0],
            filter_recv.at[i],
            device_id={"ctx": y * LINE + peer},
            device_id_type=MESH,
        ).start()
        return carry

    def across_filter(src, origin):
        for dy in range(1, ys):
            to = lax.rem(y + dy, ys)
            pltpu.make_async_remote_copy(
                src.at[to],
                h_ref.at[rows_of(y * LINE + origin, 1)],
                filter_sem.at[0],
                filter_sem.at[1],
                device_id={"ctx": to * LINE + spot},
                device_id_type=MESH,
            ).start()

    lax.fori_loop(1, LINE, along_filter, 0)
    across_filter(filter_t.at[:, spot], spot)
    h_ref[own, :] = filter_t[y, spot]
    halo.wait()

    def shortened(i, at):
        edge = jnp.where(me > 0, halo_ref[i, :, at].astype(f32), 0.0)
        wide = jnp.concatenate([edge, qkv_ref[i, :, at].astype(f32)], axis=0)
        return (
            taps_ref[i, 0:1, at] * wide[HALO:]
            + taps_ref[i, 1:2, at] * wide[HALO - 1 : HALO - 1 + tokens]
            + taps_ref[i, 2:3, at] * wide[HALO - 2 : HALO - 2 + tokens]
        )

    signal_cross = [cross(signal_t, signal_strip, signal_hop, dy) for dy in nearest]
    for dy, copy in zip(nearest + [0], signal_cross + [None]):
        at = rows_of(lax.rem(y + dy, ys) * LINE, LINE)
        signal = (shortened(1, at) * shortened(2, at)).astype(bf16)
        signal_ref[:, at] = signal
        signal_t[at, :] = signal.astype(f32).T.astype(bf16)
        if copy is not None:
            copy.start()
    along(signal_t, y * LINE, x_ref, signal_sem, y)

    def query(i, carry):
        at = chunk_at(i)
        query_ref[:, at] = shortened(0, at)
        return carry

    lax.fori_loop(0, chunks, query, 0)

    def pass_signal(index):
        dy = nearest[index]
        signal_cross[index].wait_recv()
        along(signal_strip.at[dy - 1], 0, x_ref, signal_sem, lax.rem(y + ys - dy, ys))

    for index in range(ys - 2):
        pass_signal(index)

    def pass_filter(i, carry):
        origin = lax.rem(spot + LINE - i, LINE)
        pltpu.make_async_remote_copy(
            filter_line.at[i],
            filter_line.at[i],
            filter_send.at[0],
            filter_recv.at[i],
            device_id={"ctx": me},
            device_id_type=MESH,
        ).wait_recv()
        across_filter(filter_line.at[i], origin)
        h_ref[rows_of(y * LINE + origin, 1), :] = filter_line[i, y]
        return carry

    lax.fori_loop(1, LINE, pass_filter, 0)
    pass_signal(ys - 2)

    width = tokens
    first_row = lax.broadcasted_iota(jnp.int32, (blocks, width), 0) == 0
    halves = (slice(0, half_tok), slice(half_tok, tokens))

    def turns_of():
        return twiddle_ref[0, :blocks], twiddle_ref[1, :blocks], twiddle_ref[0, blocks:], twiddle_ref[1, blocks:]

    def spectrum(ref):
        cos, sin, cos_last, sin_last = turns_of()
        for h, part in enumerate(halves):
            wide_ref[h] = ref[:, part].astype(f32)
        turned, last = [], []
        for c in range(lanes):
            picked = pl.ds(c, blocks, stride=lanes)
            column = jnp.concatenate([wide_ref[0, picked, :], wide_ref[1, picked, :]], axis=1).astype(bf16)
            first = dot(lead_ref[...], column)
            real, imag = first[:blocks], first[blocks:]
            last.append(imag[0:1])
            imag = jnp.where(first_row, 0.0, imag)
            turned.append(jnp.concatenate([real * cos - imag * sin, real * sin + imag * cos], axis=1).astype(bf16))
        last = jnp.concatenate(last, axis=0)
        turned.append(jnp.concatenate([last * cos_last, last * sin_last], axis=1).astype(bf16))
        return dot(jnp.concatenate(turned, axis=0), forward_ref[...])

    for load in loads[2:5]:
        load.wait()
    from_filter = settled(x_ref, h_ref, filter_sem, (ys - 1) * LINE)
    from_filter.wait_recv()

    sh_ref[...] = spectrum(h_ref).astype(bf16)
    for load in loads[5:]:
        load.wait()
    from_filter.wait_send()
    sent = pl.ds(0, LINE - 1)
    pltpu.make_async_remote_copy(
        filter_line.at[sent],
        filter_line.at[sent],
        filter_send.at[0],
        filter_recv.at[0],
        device_id={"ctx": me},
        device_id_type=MESH,
    ).wait_send()
    from_signal = settled(signal_t, x_ref, signal_sem, ys * (LINE - 1))
    from_signal.wait_recv()

    sx = spectrum(x_ref)
    xr, xi = sx[:, :width], sx[:, width:]
    hr, hi = sh_ref[:, :width].astype(f32), sh_ref[:, width:].astype(f32)
    product = jnp.concatenate([xr * hr - xi * hi, xr * hi + xi * hr], axis=1).astype(bf16)
    back = dot(product, backward_ref[...])
    br, bi = back[:, :width], back[:, width:]
    cos, sin, cos_last, sin_last = turns_of()
    last = br[lanes * blocks :] * cos_last + bi[lanes * blocks :] * sin_last
    for c in range(lanes):
        at = slice(c * blocks, (c + 1) * blocks)
        real, imag = br[at], bi[at]
        imag_turned = jnp.where(first_row, last[c : c + 1], imag * cos - real * sin)
        turned = jnp.concatenate([real * cos + imag * sin, imag_turned], axis=0).astype(bf16)
        y = dot(tail_ref[...], turned)
        for h, part in enumerate(halves):
            wide_ref[h, pl.ds(c, blocks, stride=lanes), :] = y[:, part]

    def send_conv(h):
        def one(i, carry):
            p = lax.rem(me + i, blocks)
            pltpu.make_async_remote_copy(
                piece(y_ref.at[h], p),
                piece(conv_ref.at[h], me),
                conv_send.at[h],
                conv_recv.at[h],
                device_id={"ctx": p},
                device_id_type=MESH,
            ).start()
            return carry

        lax.fori_loop(1, blocks, one, 0)

    for h in range(2):
        y_ref[h] = wide_ref[h].astype(bf16)
        send_conv(h)
    from_conv = []
    for h in range(2):
        conv_ref[h, own, :] = y_ref[h, own, :]
        rows_all = pl.ds(0, (blocks - 1) * lanes)
        from_conv.append(
            pltpu.make_async_remote_copy(
                y_ref.at[h, rows_all],
                conv_ref.at[h, rows_all],
                conv_send.at[h],
                conv_recv.at[h],
                device_id={"ctx": me},
                device_id_type=MESH,
            )
        )

    def tp_copy(src, dst, h, kind, side):
        s = (h * 3 + kind) * 2 + side
        return pltpu.make_async_remote_copy(
            src, dst, tp_send.at[s], tp_recv.at[s], device_id={"tp": (right, left)[side]}, device_id_type=MESH
        )

    def project(h, dest, start):
        at = pl.ds(pl.multiple_of(dest * cols + start, half_col), half_col)
        return dot(gated_ref[h], weight_ref[:, at])

    far = lax.rem(col + 2, tps)
    relays, opens, sums = [], [], []
    for h in range(2):
        from_conv[h].wait_recv()
        tok = pl.ds(h * half_tok, half_tok)

        for i in range(chunks):
            at = slice(i * LANE, (i + 1) * LANE)
            conv = conv_ref[h, at, :].astype(f32).T
            signal = signal_ref[tok, at].astype(f32)
            gated_ref[h, :, at] = (query_ref[tok, at] * (conv + skip_ref[:, at] * signal)).astype(bf16)
        for side in range(2):
            relay_src[h, side] = project(h, far, side * half_col).astype(bf16)
            copy = tp_copy(relay_src.at[h, side], relay_in.at[h, side], h, 0, side)
            copy.start()
            relays.append(copy)
        for side, dest in ((0, right), (1, left)):
            send_ref[h, side, 1] = project(h, dest, (1 - side) * half_col).astype(bf16)
            copy = tp_copy(send_ref.at[h, side, 1], take_ref.at[h, side, 1], h, 1, side)
            copy.start()
            opens.append(copy)
        for side, dest in ((0, right), (1, left)):
            part_ref[side] = project(h, dest, side * half_col)
        for side in range(2):
            relays[2 * h + side].wait_recv()
            send_ref[h, side, 0] = (part_ref[side] + relay_in[h, side].astype(f32)).astype(bf16)
            copy = tp_copy(send_ref.at[h, side, 0], take_ref.at[h, side, 0], h, 2, side)
            copy.start()
            sums.append(copy)
        for part in range(2):
            part_ref[2 + 2 * h + part] = project(h, col, part * half_col)

    for h in range(2):
        for side in range(2):
            opens[2 * h + side].wait_recv()
            sums[2 * h + side].wait_recv()
        tok = pl.ds(h * half_tok, half_tok)
        for part in range(2):
            total = (
                part_ref[2 + 2 * h + part]
                + take_ref[h, 0, part].astype(f32)
                + take_ref[h, 1, 1 - part].astype(f32)
            )
            out_ref[tok, pl.ds(part * half_col, half_col)] = total.astype(bf16)

    from_signal.wait_send()
    for copy in signal_cross + from_conv + relays + opens + sums:
        copy.wait_send()


def body(qkv, short_taps, long_filter, skip, out_weight):
    blocks = lax.axis_size("ctx")
    tps = lax.axis_size("tp")
    tokens, channels = qkv.shape[1:]
    lanes = channels // blocks
    lines = blocks // LINE
    cols = out_weight.shape[1] // tps
    consts = [jnp.asarray(c) for c in tables(blocks, tokens, lanes)]
    freqs = (blocks + 1) * lanes
    vmem = pl.BlockSpec(memory_space=pltpu.VMEM)
    hbm = pl.BlockSpec(memory_space=pl.ANY)
    bf16 = jnp.bfloat16
    f32 = jnp.float32
    dma = pltpu.SemaphoreType.DMA
    half = tokens // 2
    return pl.pallas_call(
        functools.partial(kernel, blocks, tps, lanes),
        out_shape=jax.ShapeDtypeStruct((tokens, cols), bf16),
        in_specs=[hbm, vmem, hbm, vmem] + [hbm] * 6,
        out_specs=vmem,
        scratch_shapes=[
            pltpu.VMEM(qkv.shape, bf16),
            pltpu.VMEM((tokens, channels), bf16),
            pltpu.VMEM(out_weight.shape, bf16),
            *[pltpu.VMEM(c.shape, c.dtype) for c in consts],
            pltpu.VMEM((3, HALO, channels), bf16),
            pltpu.VMEM((lines, LINE, lanes, tokens), bf16),
            pltpu.VMEM((channels, tokens), bf16),
            pltpu.VMEM((LINE, lines, lanes, tokens), bf16),
            pltpu.VMEM((lines - 1, LINE * lanes, tokens), bf16),
            pltpu.VMEM((tokens, channels), bf16),
            pltpu.VMEM((tokens, channels), f32),
            pltpu.VMEM((channels, tokens), bf16),
            pltpu.VMEM((channels, tokens), bf16),
            pltpu.VMEM((freqs, 2 * tokens), bf16),
            pltpu.VMEM((2, channels, half), f32),
            pltpu.VMEM((2, channels, half), bf16),
            pltpu.VMEM((2, channels, half), bf16),
            pltpu.VMEM((2, half, channels), bf16),
            pltpu.VMEM((2, 2, half, cols // 2), bf16),
            pltpu.VMEM((2, 2, half, cols // 2), bf16),
            pltpu.VMEM((6, half, cols // 2), f32),
            pltpu.VMEM((2, 2, 2, half, cols // 2), bf16),
            pltpu.VMEM((2, 2, 2, half, cols // 2), bf16),
            dma((8,)),
            dma((2,)),
            dma((1,)),
            dma((LINE,)),
            dma((2, lines - 1)),
            dma((2,)),
            dma((2,)),
            dma((2,)),
            dma((2,)),
            dma((12,)),
            dma((12,)),
        ],
        compiler_params=pltpu.CompilerParams(
            collective_id=0, has_side_effects=True, vmem_limit_bytes=56 << 20
        ),
        name="hyena",
    )(qkv, short_taps, long_filter, skip[None, :], out_weight, *consts)


def solution(mesh):
    placed = (P(None, "ctx", "tp"), P(None, None, "tp"), P("ctx", "tp"), P("tp"), P("tp", None))
    return jax.shard_map(body, mesh=mesh, in_specs=placed, out_specs=P("ctx", "tp"), check_vma=False)
```

```python
import functools

import jax
import jax.numpy as jnp
import numpy as np
from jax import lax
from jax.experimental import pallas as pl
from jax.experimental.pallas import tpu as pltpu
from jax.sharding import PartitionSpec as P

MESH = pl.DeviceIdType.MESH
LANE = 128
LINE = 16
HALO = 16


def tables(blocks, width, lanes):
    f = np.arange(blocks)
    points = 2 * blocks * width
    angle = 2.0 * np.pi * np.outer(f, np.arange(blocks)) / (2 * blocks)
    real, imag = np.cos(angle), -np.sin(angle)
    imag[0] = np.cos(np.pi * f)
    weight = np.where(f == 0, 1.0, 2.0)[:, None] / points
    back_real, back_imag = real * weight, imag * weight
    back_imag[0] = imag[0] / points
    turn = 2.0 * np.pi * np.outer(np.minimum(np.arange(blocks + lanes), blocks), np.arange(width)) / points
    inner = 2.0 * np.pi * np.outer(np.arange(width), np.arange(width)) / width
    c, s = np.cos(inner), np.sin(inner)
    half = jnp.bfloat16
    return (
        np.concatenate([real, imag]).astype(half),
        np.concatenate([back_real, back_imag]).T.astype(half),
        np.stack([np.cos(turn), -np.sin(turn)]).astype(np.float32),
        np.block([[c, -s], [s, c]]).astype(half),
        np.block([[c, s], [-s, c]]).astype(half),
    )


def dot(left, right):
    return jnp.dot(left, right, preferred_element_type=jnp.float32)


def kernel(
    blocks,
    tps,
    lanes,
    qkv_hbm,
    taps_ref,
    filter_hbm,
    skip_ref,
    weight_hbm,
    lead_hbm,
    tail_hbm,
    twiddle_hbm,
    forward_hbm,
    backward_hbm,
    out_ref,
    qkv_ref,
    filter_ref,
    weight_ref,
    lead_ref,
    tail_ref,
    twiddle_ref,
    forward_ref,
    backward_ref,
    halo_ref,
    filter_t,
    signal_t,
    filter_line,
    signal_strip,
    signal_ref,
    query_ref,
    h_ref,
    x_ref,
    sh_ref,
    wide_ref,
    y_ref,
    conv_ref,
    gated_ref,
    relay_src,
    relay_in,
    part_ref,
    send_ref,
    take_ref,
    load_sem,
    halo_sem,
    filter_send,
    filter_recv,
    signal_hop,
    filter_sem,
    signal_sem,
    conv_send,
    conv_recv,
    tp_send,
    tp_recv,
):
    f32 = jnp.float32
    bf16 = jnp.bfloat16
    me = lax.axis_index("ctx")
    col = lax.axis_index("tp")
    tokens, channels = filter_ref.shape
    half_tok = tokens // 2
    half_col = out_ref.shape[1] // 2
    cols = out_ref.shape[1]

    sources = (filter_hbm, qkv_hbm, lead_hbm, twiddle_hbm, forward_hbm, weight_hbm, backward_hbm, tail_hbm)
    targets = (filter_ref, qkv_ref, lead_ref, twiddle_ref, forward_ref, weight_ref, backward_ref, tail_ref)
    loads = [pltpu.make_async_copy(s, t, load_sem.at[i]) for i, (s, t) in enumerate(zip(sources, targets))]
    for load in loads:
        load.start()

    barrier = pltpu.get_barrier_semaphore()

    ys = blocks // LINE
    y = me // LINE
    spot = lax.rem(me, LINE)
    strip_rows = LINE * lanes

    def greet(i, carry):
        peer = y * LINE + lax.rem(spot + i, LINE)
        pl.semaphore_signal(barrier, inc=1, device_id={"ctx": peer}, device_id_type=MESH)
        return carry

    lax.fori_loop(1, LINE, greet, 0)
    for back_by in [LINE * dy for dy in range(1, ys)] + [1]:
        peer = lax.rem(me + blocks - back_by, blocks)
        pl.semaphore_signal(barrier, inc=1, device_id={"ctx": peer}, device_id_type=MESH)
    right = lax.rem(col + 1, tps)
    left = lax.rem(col + tps - 1, tps)
    for side in (left, right):
        pl.semaphore_signal(barrier, inc=1, device_id={"tp": side}, device_id_type=MESH)

    chunks = channels // LANE

    def piece(ref, p):
        return ref.at[pl.ds(pl.multiple_of(p * lanes, lanes), lanes)]

    def chunk_at(i):
        return pl.ds(pl.multiple_of(i * LANE, LANE), LANE)

    def rows_of(block, count):
        return pl.ds(pl.multiple_of(block * lanes, lanes), count * lanes)

    def cross(src, strip, sems, dy):
        to = lax.rem(y + dy, ys)
        return pltpu.make_async_remote_copy(
            src.at[rows_of(to * LINE, LINE)],
            strip.at[dy - 1],
            sems.at[0, dy - 1],
            sems.at[1, dy - 1],
            device_id={"ctx": to * LINE + spot},
            device_id_type=MESH,
        )

    def along(src, first, dst, sems, origin, core):
        there = rows_of(origin * LINE + spot, 1)

        def one(i, carry):
            peer = 2 * lax.rem(spot // 2 + i, LINE // 2) + core

            @pl.when(peer != spot)
            def _():
                pltpu.make_async_remote_copy(
                    src.at[rows_of(first + peer, 1)],
                    dst.at[there],
                    sems.at[0],
                    sems.at[1],
                    device_id={"ctx": y * LINE + peer},
                    device_id_type=MESH,
                ).start()

            return carry

        lax.fori_loop(0, LINE // 2, one, 0)
        if core == 0:
            dst[there, :] = src[rows_of(first + spot, 1), :]

    def settled(src, dst, sems, pieces):
        rows = pieces * lanes
        return pltpu.make_async_remote_copy(
            src.at[pl.ds(0, rows)],
            dst.at[pl.ds(0, rows)],
            sems.at[0],
            sems.at[1],
            device_id={"ctx": me},
            device_id_type=MESH,
        )

    own = rows_of(me, 1)
    nearest = sorted(range(1, ys), key=lambda dy: min(dy, ys - dy))

    loads[0].wait()

    per = LANE // lanes
    for i in range(chunks):
        turned = filter_ref[:, i * LANE : (i + 1) * LANE].astype(f32).T.astype(bf16)
        place = slice(i * per % LINE, i * per % LINE + per)
        filter_t[i * per // LINE, place] = turned.reshape(per, lanes, tokens)
    loads[1].wait()
    pl.semaphore_wait(barrier, LINE + ys + 1)

    halo = pltpu.make_async_remote_copy(
        qkv_ref.at[:, pl.ds(tokens - HALO, HALO)],
        halo_ref,
        halo_sem.at[0],
        halo_sem.at[1],
        device_id={"ctx": lax.rem(me + 1, blocks)},
        device_id_type=MESH,
    )
    halo.start()

    def along_filter(i, carry):
        peer = lax.rem(spot + i, LINE)
        pltpu.make_async_remote_copy(
            filter_t.at[:, peer],
            filter_line.at[i],
            filter_send.at[0],
            filter_recv.at[i],
            device_id={"ctx": y * LINE + peer},
            device_id_type=MESH,
        ).start()
        return carry

    def across_filter(src, origin):
        for dy in range(1, ys):
            to = lax.rem(y + dy, ys)
            pltpu.make_async_remote_copy(
                src.at[to],
                h_ref.at[rows_of(y * LINE + origin, 1)],
                filter_sem.at[0],
                filter_sem.at[1],
                device_id={"ctx": to * LINE + spot},
                device_id_type=MESH,
            ).start()

    lax.fori_loop(1, LINE, along_filter, 0)
    across_filter(filter_t.at[:, spot], spot)
    h_ref[own, :] = filter_t[y, spot]
    halo.wait()

    def shortened(i, at):
        edge = jnp.where(me > 0, halo_ref[i, :, at].astype(f32), 0.0)
        wide = jnp.concatenate([edge, qkv_ref[i, :, at].astype(f32)], axis=0)
        return (
            taps_ref[i, 0:1, at] * wide[HALO:]
            + taps_ref[i, 1:2, at] * wide[HALO - 1 : HALO - 1 + tokens]
            + taps_ref[i, 2:3, at] * wide[HALO - 2 : HALO - 2 + tokens]
        )

    signal_cross = [cross(signal_t, signal_strip, signal_hop, dy) for dy in nearest]
    for dy, copy in zip(nearest + [0], signal_cross + [None]):
        at = rows_of(lax.rem(y + dy, ys) * LINE, LINE)
        signal = (shortened(1, at) * shortened(2, at)).astype(bf16)
        signal_ref[:, at] = signal
        signal_t[at, :] = signal.astype(f32).T.astype(bf16)
        if copy is not None:
            copy.start()
    along(signal_t, y * LINE, x_ref, signal_sem, y, 0)

    def query(i, carry):
        at = chunk_at(i)
        query_ref[:, at] = shortened(0, at)
        return carry

    lax.fori_loop(0, chunks, query, 0)

    def pass_signal(index, core):
        dy = nearest[index]
        if core == 0:
            signal_cross[index].wait_recv()
        along(signal_strip.at[dy - 1], 0, x_ref, signal_sem, lax.rem(y + ys - dy, ys), core)

    for index in range(ys - 2):
        pass_signal(index, 0)

    def pass_filter(i, carry):
        origin = lax.rem(spot + LINE - i, LINE)
        pltpu.make_async_remote_copy(
            filter_line.at[i],
            filter_line.at[i],
            filter_send.at[0],
            filter_recv.at[i],
            device_id={"ctx": me},
            device_id_type=MESH,
        ).wait_recv()
        across_filter(filter_line.at[i], origin)
        h_ref[rows_of(y * LINE + origin, 1), :] = filter_line[i, y]
        return carry

    lax.fori_loop(1, LINE, pass_filter, 0)
    pass_signal(ys - 2, 0)
    along(signal_t, y * LINE, x_ref, signal_sem, y, 1)
    for index in range(ys - 1):
        pass_signal(index, 1)

    width = tokens
    first_row = lax.broadcasted_iota(jnp.int32, (blocks, width), 0) == 0
    halves = (slice(0, half_tok), slice(half_tok, tokens))

    def turns_of():
        return twiddle_ref[0, :blocks], twiddle_ref[1, :blocks], twiddle_ref[0, blocks:], twiddle_ref[1, blocks:]

    def spectrum(ref):
        cos, sin, cos_last, sin_last = turns_of()
        for h, part in enumerate(halves):
            wide_ref[h] = ref[:, part].astype(f32)
        turned, last = [], []
        for c in range(lanes):
            picked = pl.ds(c, blocks, stride=lanes)
            column = jnp.concatenate([wide_ref[0, picked, :], wide_ref[1, picked, :]], axis=1).astype(bf16)
            first = dot(lead_ref[...], column)
            real, imag = first[:blocks], first[blocks:]
            last.append(imag[0:1])
            imag = jnp.where(first_row, 0.0, imag)
            turned.append(jnp.concatenate([real * cos - imag * sin, real * sin + imag * cos], axis=1).astype(bf16))
        last = jnp.concatenate(last, axis=0)
        turned.append(jnp.concatenate([last * cos_last, last * sin_last], axis=1).astype(bf16))
        return dot(jnp.concatenate(turned, axis=0), forward_ref[...])

    for load in loads[2:5]:
        load.wait()
    from_filter = settled(x_ref, h_ref, filter_sem, (ys - 1) * LINE)
    from_filter.wait_recv()

    sh_ref[...] = spectrum(h_ref).astype(bf16)
    for load in loads[5:]:
        load.wait()
    from_filter.wait_send()
    sent = pl.ds(0, LINE - 1)
    pltpu.make_async_remote_copy(
        filter_line.at[sent],
        filter_line.at[sent],
        filter_send.at[0],
        filter_recv.at[0],
        device_id={"ctx": me},
        device_id_type=MESH,
    ).wait_send()
    from_signal = settled(signal_t, x_ref, signal_sem, ys * (LINE - 1))
    from_signal.wait_recv()

    sx = spectrum(x_ref)
    xr, xi = sx[:, :width], sx[:, width:]
    hr, hi = sh_ref[:, :width].astype(f32), sh_ref[:, width:].astype(f32)
    product = jnp.concatenate([xr * hr - xi * hi, xr * hi + xi * hr], axis=1).astype(bf16)
    back = dot(product, backward_ref[...])
    br, bi = back[:, :width], back[:, width:]
    cos, sin, cos_last, sin_last = turns_of()
    last = br[lanes * blocks :] * cos_last + bi[lanes * blocks :] * sin_last
    for c in range(lanes):
        at = slice(c * blocks, (c + 1) * blocks)
        real, imag = br[at], bi[at]
        imag_turned = jnp.where(first_row, last[c : c + 1], imag * cos - real * sin)
        turned = jnp.concatenate([real * cos + imag * sin, imag_turned], axis=0).astype(bf16)
        y = dot(tail_ref[...], turned)
        for h, part in enumerate(halves):
            wide_ref[h, pl.ds(c, blocks, stride=lanes), :] = y[:, part]

    def send_conv(h):
        def one(i, carry):
            p = lax.rem(me + i, blocks)
            pltpu.make_async_remote_copy(
                piece(y_ref.at[h], p),
                piece(conv_ref.at[h], me),
                conv_send.at[h],
                conv_recv.at[h],
                device_id={"ctx": p},
                device_id_type=MESH,
            ).start()
            return carry

        lax.fori_loop(1, blocks, one, 0)

    y_ref[0] = wide_ref[0].astype(bf16)
    send_conv(0)
    y_ref[1] = wide_ref[1].astype(bf16)
    from_conv = []
    for h in range(2):
        conv_ref[h, own, :] = y_ref[h, own, :]
        rows_all = pl.ds(0, (blocks - 1) * lanes)
        from_conv.append(
            pltpu.make_async_remote_copy(
                y_ref.at[h, rows_all],
                conv_ref.at[h, rows_all],
                conv_send.at[h],
                conv_recv.at[h],
                device_id={"ctx": me},
                device_id_type=MESH,
            )
        )

    def tp_copy(src, dst, h, kind, side):
        s = (h * 3 + kind) * 2 + side
        return pltpu.make_async_remote_copy(
            src, dst, tp_send.at[s], tp_recv.at[s], device_id={"tp": (right, left)[side]}, device_id_type=MESH
        )

    def project(h, dest, start):
        at = pl.ds(pl.multiple_of(dest * cols + start, half_col), half_col)
        return dot(gated_ref[h], weight_ref[:, at])

    far = lax.rem(col + 2, tps)
    relays, opens, sums = {}, {}, {}

    def gate(h):
        tok = pl.ds(h * half_tok, half_tok)
        for i in range(chunks):
            at = slice(i * LANE, (i + 1) * LANE)
            conv = conv_ref[h, at, :].astype(f32).T
            signal = signal_ref[tok, at].astype(f32)
            gated_ref[h, :, at] = (query_ref[tok, at] * (conv + skip_ref[:, at] * signal)).astype(bf16)

    def relay(h):
        for side in range(2):
            relay_src[h, side] = project(h, far, side * half_col).astype(bf16)
            relays[h, side] = tp_copy(relay_src.at[h, side], relay_in.at[h, side], h, 0, side)
            relays[h, side].start()

    def give(h):
        for side, dest in ((0, right), (1, left)):
            send_ref[h, side, 1] = project(h, dest, (1 - side) * half_col).astype(bf16)
            opens[h, side] = tp_copy(send_ref.at[h, side, 1], take_ref.at[h, side, 1], h, 1, side)
            opens[h, side].start()

    def meet(h):
        for side, dest in ((0, right), (1, left)):
            part_ref[h, side] = project(h, dest, side * half_col)

    def add(h):
        for side in range(2):
            relays[h, side].wait_recv()
            send_ref[h, side, 0] = (part_ref[h, side] + relay_in[h, side].astype(f32)).astype(bf16)
            sums[h, side] = tp_copy(send_ref.at[h, side, 0], take_ref.at[h, side, 0], h, 2, side)
            sums[h, side].start()

    def keep(h):
        for part in range(2):
            part_ref[h, 2 + part] = project(h, col, part * half_col)

    for h in range(2):
        from_conv[h].wait_recv()
        if h == 0:
            send_conv(1)
        gate(h)
        relay(h)
        give(h)
        meet(h)
        add(h)
        keep(h)

    for h in range(2):
        for side in range(2):
            opens[h, side].wait_recv()
            sums[h, side].wait_recv()
        tok = pl.ds(h * half_tok, half_tok)
        for part in range(2):
            total = (
                part_ref[h, 2 + part]
                + take_ref[h, 0, part].astype(f32)
                + take_ref[h, 1, 1 - part].astype(f32)
            )
            out_ref[tok, pl.ds(part * half_col, half_col)] = total.astype(bf16)

    from_signal.wait_send()
    for copy in [*signal_cross, *from_conv, *relays.values(), *opens.values(), *sums.values()]:
        copy.wait_send()


def body(qkv, short_taps, long_filter, skip, out_weight):
    blocks = lax.axis_size("ctx")
    tps = lax.axis_size("tp")
    tokens, channels = qkv.shape[1:]
    lanes = channels // blocks
    lines = blocks // LINE
    cols = out_weight.shape[1] // tps
    consts = [jnp.asarray(c) for c in tables(blocks, tokens, lanes)]
    freqs = (blocks + 1) * lanes
    vmem = pl.BlockSpec(memory_space=pltpu.VMEM)
    hbm = pl.BlockSpec(memory_space=pl.ANY)
    bf16 = jnp.bfloat16
    f32 = jnp.float32
    dma = pltpu.SemaphoreType.DMA
    half = tokens // 2
    return pl.pallas_call(
        functools.partial(kernel, blocks, tps, lanes),
        out_shape=jax.ShapeDtypeStruct((tokens, cols), bf16),
        in_specs=[hbm, vmem, hbm, vmem] + [hbm] * 6,
        out_specs=vmem,
        scratch_shapes=[
            pltpu.VMEM(qkv.shape, bf16),
            pltpu.VMEM((tokens, channels), bf16),
            pltpu.VMEM(out_weight.shape, bf16),
            *[pltpu.VMEM(c.shape, c.dtype) for c in consts],
            pltpu.VMEM((3, HALO, channels), bf16),
            pltpu.VMEM((lines, LINE, lanes, tokens), bf16),
            pltpu.VMEM((channels, tokens), bf16),
            pltpu.VMEM((LINE, lines, lanes, tokens), bf16),
            pltpu.VMEM((lines - 1, LINE * lanes, tokens), bf16),
            pltpu.VMEM((tokens, channels), bf16),
            pltpu.VMEM((tokens, channels), f32),
            pltpu.VMEM((channels, tokens), bf16),
            pltpu.VMEM((channels, tokens), bf16),
            pltpu.VMEM((freqs, 2 * tokens), bf16),
            pltpu.VMEM((2, channels, half), f32),
            pltpu.VMEM((2, channels, half), bf16),
            pltpu.VMEM((2, channels, half), bf16),
            pltpu.VMEM((2, half, channels), bf16),
            pltpu.VMEM((2, 2, half, cols // 2), bf16),
            pltpu.VMEM((2, 2, half, cols // 2), bf16),
            pltpu.VMEM((2, 4, half, cols // 2), f32),
            pltpu.VMEM((2, 2, 2, half, cols // 2), bf16),
            pltpu.VMEM((2, 2, 2, half, cols // 2), bf16),
            dma((8,)),
            dma((2,)),
            dma((1,)),
            dma((LINE,)),
            dma((2, lines - 1)),
            dma((2,)),
            dma((2,)),
            dma((2,)),
            dma((2,)),
            dma((12,)),
            dma((12,)),
        ],
        compiler_params=pltpu.CompilerParams(
            collective_id=0, has_side_effects=True, vmem_limit_bytes=56 << 20
        ),
        name="hyena",
    )(qkv, short_taps, long_filter, skip[None, :], out_weight, *consts)


def solution(mesh):
    placed = (P(None, "ctx", "tp"), P(None, None, "tp"), P("ctx", "tp"), P("tp"), P("tp", None))
    return jax.shard_map(body, mesh=mesh, in_specs=placed, out_specs=P("ctx", "tp"), check_vma=False)
```

```python
import functools

import jax
import jax.numpy as jnp
import numpy as np
from jax import lax
from jax.experimental import pallas as pl
from jax.experimental.pallas import tpu as pltpu
from jax.sharding import PartitionSpec as P

MESH = pl.DeviceIdType.MESH
LANE = 128
LINE = 16
HALO = 16


def tables(blocks, width, lanes):
    f = np.arange(blocks)
    points = 2 * blocks * width
    angle = 2.0 * np.pi * np.outer(f, np.arange(blocks)) / (2 * blocks)
    real, imag = np.cos(angle), -np.sin(angle)
    imag[0] = np.cos(np.pi * f)
    weight = np.where(f == 0, 1.0, 2.0)[:, None] / points
    back_real, back_imag = real * weight, imag * weight
    back_imag[0] = imag[0] / points
    turn = 2.0 * np.pi * np.outer(np.minimum(np.arange(blocks + lanes), blocks), np.arange(width)) / points
    inner = 2.0 * np.pi * np.outer(np.arange(width), np.arange(width)) / width
    c, s = np.cos(inner), np.sin(inner)
    backward = np.block([[c, s], [-s, c]]).reshape(2 * width, 2, 2, width // 2).transpose(0, 2, 1, 3)
    backward = backward.reshape(2 * width, 2 * width)
    half = jnp.bfloat16
    return (
        np.concatenate([real, imag]).astype(half),
        np.concatenate([back_real, back_imag]).T.astype(half),
        np.stack([np.cos(turn), -np.sin(turn)]).astype(np.float32),
        np.block([[c, -s], [s, c]]).astype(half),
        backward.astype(half),
    )


def dot(left, right):
    return jnp.dot(left, right, preferred_element_type=jnp.float32)


def kernel(
    blocks,
    tps,
    lanes,
    qkv_hbm,
    taps_ref,
    filter_hbm,
    skip_ref,
    weight_hbm,
    lead_hbm,
    tail_hbm,
    twiddle_hbm,
    forward_hbm,
    backward_hbm,
    out_ref,
    qkv_ref,
    filter_ref,
    weight_ref,
    lead_ref,
    tail_ref,
    twiddle_ref,
    forward_ref,
    backward_ref,
    halo_ref,
    filter_t,
    signal_t,
    filter_line,
    signal_strip,
    signal_ref,
    query_ref,
    h_ref,
    x_ref,
    sh_ref,
    wide_ref,
    y_ref,
    conv_ref,
    gated_ref,
    relay_src,
    relay_in,
    part_ref,
    send_ref,
    take_ref,
    load_sem,
    halo_sem,
    filter_send,
    filter_recv,
    signal_hop,
    filter_sem,
    signal_sem,
    conv_send,
    conv_recv,
    tp_send,
    tp_recv,
):
    f32 = jnp.float32
    bf16 = jnp.bfloat16
    me = lax.axis_index("ctx")
    col = lax.axis_index("tp")
    tokens, channels = filter_ref.shape
    half_tok = tokens // 2
    half_col = out_ref.shape[1] // 2
    cols = out_ref.shape[1]

    sources = (filter_hbm, qkv_hbm, lead_hbm, twiddle_hbm, forward_hbm, weight_hbm, backward_hbm, tail_hbm)
    targets = (filter_ref, qkv_ref, lead_ref, twiddle_ref, forward_ref, weight_ref, backward_ref, tail_ref)
    loads = [pltpu.make_async_copy(s, t, load_sem.at[i]) for i, (s, t) in enumerate(zip(sources, targets))]
    for load in loads:
        load.start()

    barrier = pltpu.get_barrier_semaphore()

    ys = blocks // LINE
    y = me // LINE
    spot = lax.rem(me, LINE)
    strip_rows = LINE * lanes

    def greet(i, carry):
        peer = y * LINE + lax.rem(spot + i, LINE)
        pl.semaphore_signal(barrier, inc=1, device_id={"ctx": peer}, device_id_type=MESH)
        return carry

    lax.fori_loop(1, LINE, greet, 0)
    for back_by in [LINE * dy for dy in range(1, ys)] + [1]:
        peer = lax.rem(me + blocks - back_by, blocks)
        pl.semaphore_signal(barrier, inc=1, device_id={"ctx": peer}, device_id_type=MESH)
    right = lax.rem(col + 1, tps)
    left = lax.rem(col + tps - 1, tps)
    for side in (left, right):
        pl.semaphore_signal(barrier, inc=1, device_id={"tp": side}, device_id_type=MESH)

    chunks = channels // LANE

    def piece(ref, p):
        return ref.at[pl.ds(pl.multiple_of(p * lanes, lanes), lanes)]

    def chunk_at(i):
        return pl.ds(pl.multiple_of(i * LANE, LANE), LANE)

    def rows_of(block, count):
        return pl.ds(pl.multiple_of(block * lanes, lanes), count * lanes)

    def cross(src, strip, sems, dy):
        to = lax.rem(y + dy, ys)
        return pltpu.make_async_remote_copy(
            src.at[rows_of(to * LINE, LINE)],
            strip.at[dy - 1],
            sems.at[0, dy - 1],
            sems.at[1, dy - 1],
            device_id={"ctx": to * LINE + spot},
            device_id_type=MESH,
        )

    def along(src, first, dst, sems, origin, core):
        there = rows_of(origin * LINE + spot, 1)

        def one(i, carry):
            peer = 2 * lax.rem(spot // 2 + i, LINE // 2) + core

            @pl.when(peer != spot)
            def _():
                pltpu.make_async_remote_copy(
                    src.at[rows_of(first + peer, 1)],
                    dst.at[there],
                    sems.at[0],
                    sems.at[1],
                    device_id={"ctx": y * LINE + peer},
                    device_id_type=MESH,
                ).start()

            return carry

        lax.fori_loop(0, LINE // 2, one, 0)
        if core == 0:
            dst[there, :] = src[rows_of(first + spot, 1), :]

    def settled(src, dst, sems, pieces):
        rows = pieces * lanes
        return pltpu.make_async_remote_copy(
            src.at[pl.ds(0, rows)],
            dst.at[pl.ds(0, rows)],
            sems.at[0],
            sems.at[1],
            device_id={"ctx": me},
            device_id_type=MESH,
        )

    own = rows_of(me, 1)
    nearest = sorted(range(1, ys), key=lambda dy: min(dy, ys - dy))

    loads[0].wait()

    per = LANE // lanes
    for i in range(chunks):
        turned = filter_ref[:, i * LANE : (i + 1) * LANE].astype(f32).T.astype(bf16)
        place = slice(i * per % LINE, i * per % LINE + per)
        filter_t[i * per // LINE, place] = turned.reshape(per, lanes, tokens)
    loads[1].wait()
    pl.semaphore_wait(barrier, LINE + ys + 1)

    halo = pltpu.make_async_remote_copy(
        qkv_ref.at[:, pl.ds(tokens - HALO, HALO)],
        halo_ref,
        halo_sem.at[0],
        halo_sem.at[1],
        device_id={"ctx": lax.rem(me + 1, blocks)},
        device_id_type=MESH,
    )
    halo.start()

    def along_filter(i, carry):
        peer = lax.rem(spot + i, LINE)
        pltpu.make_async_remote_copy(
            filter_t.at[:, peer],
            filter_line.at[i],
            filter_send.at[0],
            filter_recv.at[i],
            device_id={"ctx": y * LINE + peer},
            device_id_type=MESH,
        ).start()
        return carry

    def across_filter(src, origin):
        for dy in range(1, ys):
            to = lax.rem(y + dy, ys)
            pltpu.make_async_remote_copy(
                src.at[to],
                h_ref.at[rows_of(y * LINE + origin, 1)],
                filter_sem.at[0],
                filter_sem.at[1],
                device_id={"ctx": to * LINE + spot},
                device_id_type=MESH,
            ).start()

    lax.fori_loop(1, LINE, along_filter, 0)
    across_filter(filter_t.at[:, spot], spot)
    h_ref[own, :] = filter_t[y, spot]
    halo.wait()

    def shortened(i, at):
        edge = jnp.where(me > 0, halo_ref[i, :, at].astype(f32), 0.0)
        wide = jnp.concatenate([edge, qkv_ref[i, :, at].astype(f32)], axis=0)
        return (
            taps_ref[i, 0:1, at] * wide[HALO:]
            + taps_ref[i, 1:2, at] * wide[HALO - 1 : HALO - 1 + tokens]
            + taps_ref[i, 2:3, at] * wide[HALO - 2 : HALO - 2 + tokens]
        )

    signal_cross = [cross(signal_t, signal_strip, signal_hop, dy) for dy in nearest]
    for dy, copy in zip(nearest + [0], signal_cross + [None]):
        at = rows_of(lax.rem(y + dy, ys) * LINE, LINE)
        signal = (shortened(1, at) * shortened(2, at)).astype(bf16)
        signal_ref[:, at] = signal
        signal_t[at, :] = signal.astype(f32).T.astype(bf16)
        if copy is not None:
            copy.start()
    along(signal_t, y * LINE, x_ref, signal_sem, y, 0)

    def query(i, carry):
        at = chunk_at(i)
        query_ref[:, at] = shortened(0, at)
        return carry

    lax.fori_loop(0, chunks, query, 0)

    def pass_signal(index, core):
        dy = nearest[index]
        if core == 0:
            signal_cross[index].wait_recv()
        along(signal_strip.at[dy - 1], 0, x_ref, signal_sem, lax.rem(y + ys - dy, ys), core)

    for index in range(ys - 2):
        pass_signal(index, 0)

    def pass_filter(i, carry):
        origin = lax.rem(spot + LINE - i, LINE)
        pltpu.make_async_remote_copy(
            filter_line.at[i],
            filter_line.at[i],
            filter_send.at[0],
            filter_recv.at[i],
            device_id={"ctx": me},
            device_id_type=MESH,
        ).wait_recv()
        across_filter(filter_line.at[i], origin)
        h_ref[rows_of(y * LINE + origin, 1), :] = filter_line[i, y]
        return carry

    lax.fori_loop(1, LINE, pass_filter, 0)
    pass_signal(ys - 2, 0)
    along(signal_t, y * LINE, x_ref, signal_sem, y, 1)
    for index in range(ys - 1):
        pass_signal(index, 1)

    width = tokens
    first_row = lax.broadcasted_iota(jnp.int32, (blocks, width), 0) == 0
    halves = (slice(0, half_tok), slice(half_tok, tokens))

    def turns_of():
        return twiddle_ref[0, :blocks], twiddle_ref[1, :blocks], twiddle_ref[0, blocks:], twiddle_ref[1, blocks:]

    def spectrum(ref):
        cos, sin, cos_last, sin_last = turns_of()
        for h, part in enumerate(halves):
            wide_ref[h] = ref[:, part].astype(f32)
        turned, last = [], []
        for c in range(lanes):
            picked = pl.ds(c, blocks, stride=lanes)
            column = jnp.concatenate([wide_ref[0, picked, :], wide_ref[1, picked, :]], axis=1).astype(bf16)
            first = dot(lead_ref[...], column)
            real, imag = first[:blocks], first[blocks:]
            last.append(imag[0:1])
            imag = jnp.where(first_row, 0.0, imag)
            turned.append(jnp.concatenate([real * cos - imag * sin, real * sin + imag * cos], axis=1).astype(bf16))
        last = jnp.concatenate(last, axis=0)
        turned.append(jnp.concatenate([last * cos_last, last * sin_last], axis=1).astype(bf16))
        return dot(jnp.concatenate(turned, axis=0), forward_ref[...])

    for load in loads[2:5]:
        load.wait()
    from_filter = settled(x_ref, h_ref, filter_sem, (ys - 1) * LINE)
    from_filter.wait_recv()

    sh_ref[...] = spectrum(h_ref).astype(bf16)
    for load in loads[5:]:
        load.wait()
    from_filter.wait_send()
    sent = pl.ds(0, LINE - 1)
    pltpu.make_async_remote_copy(
        filter_line.at[sent],
        filter_line.at[sent],
        filter_send.at[0],
        filter_recv.at[0],
        device_id={"ctx": me},
        device_id_type=MESH,
    ).wait_send()
    from_signal = settled(signal_t, x_ref, signal_sem, ys * (LINE - 1))
    from_signal.wait_recv()

    sx = spectrum(x_ref)
    xr, xi = sx[:, :width], sx[:, width:]
    hr, hi = sh_ref[:, :width].astype(f32), sh_ref[:, width:].astype(f32)
    product = jnp.concatenate([xr * hr - xi * hi, xr * hi + xi * hr], axis=1).astype(bf16)
    cos, sin, cos_last, sin_last = turns_of()

    def invert(h):
        part = halves[h]
        back = dot(product, backward_ref[:, h * tokens : (h + 1) * tokens])
        br, bi = back[:, :half_tok], back[:, half_tok:]
        last = br[lanes * blocks :] * cos_last[:, part] + bi[lanes * blocks :] * sin_last[:, part]
        for c in range(lanes):
            at = slice(c * blocks, (c + 1) * blocks)
            real, imag = br[at], bi[at]
            imag_turned = jnp.where(first_row[:, part], last[c : c + 1], imag * cos[:, part] - real * sin[:, part])
            turned = jnp.concatenate([real * cos[:, part] + imag * sin[:, part], imag_turned], axis=0).astype(bf16)
            wide_ref[h, pl.ds(c, blocks, stride=lanes), :] = dot(tail_ref[...], turned)
        y_ref[h] = wide_ref[h].astype(bf16)

    waves = ((1, LINE + 1), (LINE + 1, blocks))

    def send_conv(h):
        for wave, (start, stop) in enumerate(waves):

            def one(i, carry, slot=2 * h + wave):
                p = lax.rem(me + i, blocks)
                pltpu.make_async_remote_copy(
                    piece(y_ref.at[h], p),
                    piece(conv_ref.at[h], me),
                    conv_send.at[slot],
                    conv_recv.at[slot],
                    device_id={"ctx": p},
                    device_id_type=MESH,
                ).start()
                return carry

            lax.fori_loop(start, stop, one, 0)

    invert(0)
    send_conv(0)
    invert(1)
    from_conv = []
    for h in range(2):
        conv_ref[h, own, :] = y_ref[h, own, :]
        for wave, (start, stop) in enumerate(waves):
            some = pl.ds(0, (stop - start) * lanes)
            from_conv.append(
                pltpu.make_async_remote_copy(
                    y_ref.at[h, some],
                    conv_ref.at[h, some],
                    conv_send.at[2 * h + wave],
                    conv_recv.at[2 * h + wave],
                    device_id={"ctx": me},
                    device_id_type=MESH,
                )
            )

    def tp_copy(src, dst, h, kind, side):
        s = (h * 3 + kind) * 2 + side
        return pltpu.make_async_remote_copy(
            src, dst, tp_send.at[s], tp_recv.at[s], device_id={"tp": (right, left)[side]}, device_id_type=MESH
        )

    def project(h, dest, start):
        at = pl.ds(pl.multiple_of(dest * cols + start, half_col), half_col)
        return dot(gated_ref[h], weight_ref[:, at])

    far = lax.rem(col + 2, tps)
    relays, opens, sums = {}, {}, {}

    def gate(h):
        tok = pl.ds(h * half_tok, half_tok)
        for i in range(chunks):
            at = slice(i * LANE, (i + 1) * LANE)
            conv = conv_ref[h, at, :].astype(f32).T
            signal = signal_ref[tok, at].astype(f32)
            gated_ref[h, :, at] = (query_ref[tok, at] * (conv + skip_ref[:, at] * signal)).astype(bf16)

    def relay(h):
        for side in range(2):
            relay_src[h, side] = project(h, far, side * half_col).astype(bf16)
            relays[h, side] = tp_copy(relay_src.at[h, side], relay_in.at[h, side], h, 0, side)
            relays[h, side].start()

    def give(h):
        for side, dest in ((0, right), (1, left)):
            send_ref[h, side, 1] = project(h, dest, (1 - side) * half_col).astype(bf16)
            opens[h, side] = tp_copy(send_ref.at[h, side, 1], take_ref.at[h, side, 1], h, 1, side)
            opens[h, side].start()

    def meet(h):
        for side, dest in ((0, right), (1, left)):
            part_ref[h, side] = project(h, dest, side * half_col)

    def add(h):
        for side in range(2):
            relays[h, side].wait_recv()
            send_ref[h, side, 0] = (part_ref[h, side] + relay_in[h, side].astype(f32)).astype(bf16)
            sums[h, side] = tp_copy(send_ref.at[h, side, 0], take_ref.at[h, side, 0], h, 2, side)
            sums[h, side].start()

    def keep(h):
        for part in range(2):
            part_ref[h, 2 + part] = project(h, col, part * half_col)

    for h in range(2):
        from_conv[2 * h].wait_recv()
        if h == 0:
            send_conv(1)
        from_conv[2 * h + 1].wait_recv()
        gate(h)
        relay(h)
        give(h)
        meet(h)
        add(h)
        keep(h)

    for h in range(2):
        for side in range(2):
            opens[h, side].wait_recv()
            sums[h, side].wait_recv()
        tok = pl.ds(h * half_tok, half_tok)
        for part in range(2):
            total = (
                part_ref[h, 2 + part]
                + take_ref[h, 0, part].astype(f32)
                + take_ref[h, 1, 1 - part].astype(f32)
            )
            out_ref[tok, pl.ds(part * half_col, half_col)] = total.astype(bf16)

    from_signal.wait_send()
    for copy in [*signal_cross, *from_conv, *relays.values(), *opens.values(), *sums.values()]:
        copy.wait_send()


def body(qkv, short_taps, long_filter, skip, out_weight):
    blocks = lax.axis_size("ctx")
    tps = lax.axis_size("tp")
    tokens, channels = qkv.shape[1:]
    lanes = channels // blocks
    lines = blocks // LINE
    cols = out_weight.shape[1] // tps
    consts = [jnp.asarray(c) for c in tables(blocks, tokens, lanes)]
    freqs = (blocks + 1) * lanes
    vmem = pl.BlockSpec(memory_space=pltpu.VMEM)
    hbm = pl.BlockSpec(memory_space=pl.ANY)
    bf16 = jnp.bfloat16
    f32 = jnp.float32
    dma = pltpu.SemaphoreType.DMA
    half = tokens // 2
    return pl.pallas_call(
        functools.partial(kernel, blocks, tps, lanes),
        out_shape=jax.ShapeDtypeStruct((tokens, cols), bf16),
        in_specs=[hbm, vmem, hbm, vmem] + [hbm] * 6,
        out_specs=vmem,
        scratch_shapes=[
            pltpu.VMEM(qkv.shape, bf16),
            pltpu.VMEM((tokens, channels), bf16),
            pltpu.VMEM(out_weight.shape, bf16),
            *[pltpu.VMEM(c.shape, c.dtype) for c in consts],
            pltpu.VMEM((3, HALO, channels), bf16),
            pltpu.VMEM((lines, LINE, lanes, tokens), bf16),
            pltpu.VMEM((channels, tokens), bf16),
            pltpu.VMEM((LINE, lines, lanes, tokens), bf16),
            pltpu.VMEM((lines - 1, LINE * lanes, tokens), bf16),
            pltpu.VMEM((tokens, channels), bf16),
            pltpu.VMEM((tokens, channels), f32),
            pltpu.VMEM((channels, tokens), bf16),
            pltpu.VMEM((channels, tokens), bf16),
            pltpu.VMEM((freqs, 2 * tokens), bf16),
            pltpu.VMEM((2, channels, half), f32),
            pltpu.VMEM((2, channels, half), bf16),
            pltpu.VMEM((2, channels, half), bf16),
            pltpu.VMEM((2, half, channels), bf16),
            pltpu.VMEM((2, 2, half, cols // 2), bf16),
            pltpu.VMEM((2, 2, half, cols // 2), bf16),
            pltpu.VMEM((2, 4, half, cols // 2), f32),
            pltpu.VMEM((2, 2, 2, half, cols // 2), bf16),
            pltpu.VMEM((2, 2, 2, half, cols // 2), bf16),
            dma((8,)),
            dma((2,)),
            dma((1,)),
            dma((LINE,)),
            dma((2, lines - 1)),
            dma((2,)),
            dma((2,)),
            dma((4,)),
            dma((4,)),
            dma((12,)),
            dma((12,)),
        ],
        compiler_params=pltpu.CompilerParams(
            collective_id=0, has_side_effects=True, vmem_limit_bytes=56 << 20
        ),
        name="hyena",
    )(qkv, short_taps, long_filter, skip[None, :], out_weight, *consts)


def solution(mesh):
    placed = (P(None, "ctx", "tp"), P(None, None, "tp"), P("ctx", "tp"), P("tp"), P("tp", None))
    return jax.shard_map(body, mesh=mesh, in_specs=placed, out_specs=P("ctx", "tp"), check_vma=False)
```

```python
import functools

import jax
import jax.numpy as jnp
import numpy as np
from jax import lax
from jax.experimental import pallas as pl
from jax.experimental.pallas import tpu as pltpu
from jax.sharding import PartitionSpec as P

MESH = pl.DeviceIdType.MESH
LANE = 128
LINE = 16
HALO = 16


def tables(blocks, width, lanes):
    f = np.arange(blocks)
    points = 2 * blocks * width
    angle = 2.0 * np.pi * np.outer(f, np.arange(blocks)) / (2 * blocks)
    real, imag = np.cos(angle), -np.sin(angle)
    imag[0] = np.cos(np.pi * f)
    weight = np.where(f == 0, 1.0, 2.0)[:, None] / points
    back_real, back_imag = real * weight, imag * weight
    back_imag[0] = imag[0] / points
    turn = 2.0 * np.pi * np.outer(np.minimum(np.arange(blocks + lanes), blocks), np.arange(width)) / points
    inner = 2.0 * np.pi * np.outer(np.arange(width), np.arange(width)) / width
    c, s = np.cos(inner), np.sin(inner)
    backward = np.block([[c, s], [-s, c]]).reshape(2 * width, 2, 2, width // 2).transpose(0, 2, 1, 3)
    backward = backward.reshape(2 * width, 2 * width)
    half = jnp.bfloat16
    return (
        np.concatenate([real, imag]).astype(half),
        np.concatenate([back_real, back_imag]).T.astype(half),
        np.stack([np.cos(turn), -np.sin(turn)]).astype(np.float32),
        np.block([[c, -s], [s, c]]).astype(half),
        backward.astype(half),
    )


def dot(left, right):
    return jnp.dot(left, right, preferred_element_type=jnp.float32)


def kernel(
    blocks,
    tps,
    lanes,
    qkv_hbm,
    taps_ref,
    filter_hbm,
    skip_ref,
    weight_hbm,
    lead_hbm,
    tail_hbm,
    twiddle_hbm,
    forward_hbm,
    backward_hbm,
    out_ref,
    qkv_ref,
    filter_ref,
    weight_ref,
    lead_ref,
    tail_ref,
    twiddle_ref,
    forward_ref,
    backward_ref,
    halo_ref,
    filter_t,
    signal_t,
    filter_line,
    signal_strip,
    signal_ref,
    query_ref,
    h_ref,
    x_ref,
    sh_ref,
    wide_ref,
    y_ref,
    conv_ref,
    gated_ref,
    relay_src,
    relay_in,
    part_ref,
    send_ref,
    take_ref,
    load_sem,
    halo_sem,
    filter_send,
    filter_recv,
    signal_hop,
    filter_sem,
    signal_sem,
    conv_send,
    conv_recv,
    tp_send,
    tp_recv,
):
    f32 = jnp.float32
    bf16 = jnp.bfloat16
    me = lax.axis_index("ctx")
    col = lax.axis_index("tp")
    tokens, channels = filter_ref.shape
    half_tok = tokens // 2
    half_col = out_ref.shape[1] // 2
    cols = out_ref.shape[1]

    sources = (filter_hbm, qkv_hbm, lead_hbm, twiddle_hbm, forward_hbm, weight_hbm, backward_hbm, tail_hbm)
    targets = (filter_ref, qkv_ref, lead_ref, twiddle_ref, forward_ref, weight_ref, backward_ref, tail_ref)
    loads = [pltpu.make_async_copy(s, t, load_sem.at[i]) for i, (s, t) in enumerate(zip(sources, targets))]
    for load in loads:
        load.start()

    barrier = pltpu.get_barrier_semaphore()

    ys = blocks // LINE
    y = me // LINE
    spot = lax.rem(me, LINE)
    strip_rows = LINE * lanes

    def greet(i, carry):
        peer = y * LINE + lax.rem(spot + i, LINE)
        pl.semaphore_signal(barrier, inc=1, device_id={"ctx": peer}, device_id_type=MESH)
        return carry

    lax.fori_loop(1, LINE, greet, 0)
    for back_by in [LINE * dy for dy in range(1, ys)] + [1]:
        peer = lax.rem(me + blocks - back_by, blocks)
        pl.semaphore_signal(barrier, inc=1, device_id={"ctx": peer}, device_id_type=MESH)
    right = lax.rem(col + 1, tps)
    left = lax.rem(col + tps - 1, tps)
    for side in (left, right):
        pl.semaphore_signal(barrier, inc=1, device_id={"tp": side}, device_id_type=MESH)

    chunks = channels // LANE

    def piece(ref, p):
        return ref.at[pl.ds(pl.multiple_of(p * lanes, lanes), lanes)]

    def chunk_at(i):
        return pl.ds(pl.multiple_of(i * LANE, LANE), LANE)

    def rows_of(block, count):
        return pl.ds(pl.multiple_of(block * lanes, lanes), count * lanes)

    def cross(src, strip, sems, dy):
        to = lax.rem(y + dy, ys)
        return pltpu.make_async_remote_copy(
            src.at[rows_of(to * LINE, LINE)],
            strip.at[dy - 1],
            sems.at[0, dy - 1],
            sems.at[1, dy - 1],
            device_id={"ctx": to * LINE + spot},
            device_id_type=MESH,
        )

    def along(src, first, dst, sems, origin, core):
        there = rows_of(origin * LINE + spot, 1)

        def one(i, carry):
            peer = 2 * lax.rem(spot // 2 + i, LINE // 2) + core

            @pl.when(peer != spot)
            def _():
                pltpu.make_async_remote_copy(
                    src.at[rows_of(first + peer, 1)],
                    dst.at[there],
                    sems.at[0],
                    sems.at[1],
                    device_id={"ctx": y * LINE + peer},
                    device_id_type=MESH,
                ).start()

            return carry

        lax.fori_loop(0, LINE // 2, one, 0)
        if core == 0:
            dst[there, :] = src[rows_of(first + spot, 1), :]

    def settled(src, dst, sems, pieces):
        rows = pieces * lanes
        return pltpu.make_async_remote_copy(
            src.at[pl.ds(0, rows)],
            dst.at[pl.ds(0, rows)],
            sems.at[0],
            sems.at[1],
            device_id={"ctx": me},
            device_id_type=MESH,
        )

    own = rows_of(me, 1)
    nearest = sorted(range(1, ys), key=lambda dy: min(dy, ys - dy))

    loads[0].wait()

    per = LANE // lanes
    for i in range(chunks):
        turned = filter_ref[:, i * LANE : (i + 1) * LANE].astype(f32).T.astype(bf16)
        place = slice(i * per % LINE, i * per % LINE + per)
        filter_t[i * per // LINE, place] = turned.reshape(per, lanes, tokens)
    loads[1].wait()
    pl.semaphore_wait(barrier, LINE + ys + 1)

    halo = pltpu.make_async_remote_copy(
        qkv_ref.at[:, pl.ds(tokens - HALO, HALO)],
        halo_ref,
        halo_sem.at[0],
        halo_sem.at[1],
        device_id={"ctx": lax.rem(me + 1, blocks)},
        device_id_type=MESH,
    )
    halo.start()

    def along_filter(i, carry):
        peer = lax.rem(spot + i, LINE)
        pltpu.make_async_remote_copy(
            filter_t.at[:, peer],
            filter_line.at[i],
            filter_send.at[0],
            filter_recv.at[i],
            device_id={"ctx": y * LINE + peer},
            device_id_type=MESH,
        ).start()
        return carry

    def across_filter(src, origin):
        for dy in range(1, ys):
            to = lax.rem(y + dy, ys)
            pltpu.make_async_remote_copy(
                src.at[to],
                h_ref.at[rows_of(y * LINE + origin, 1)],
                filter_sem.at[0],
                filter_sem.at[1],
                device_id={"ctx": to * LINE + spot},
                device_id_type=MESH,
            ).start()

    lax.fori_loop(1, LINE, along_filter, 0)
    across_filter(filter_t.at[:, spot], spot)
    h_ref[own, :] = filter_t[y, spot]
    halo.wait()

    def shortened(i, at):
        edge = jnp.where(me > 0, halo_ref[i, :, at].astype(f32), 0.0)
        wide = jnp.concatenate([edge, qkv_ref[i, :, at].astype(f32)], axis=0)
        return (
            taps_ref[i, 0:1, at] * wide[HALO:]
            + taps_ref[i, 1:2, at] * wide[HALO - 1 : HALO - 1 + tokens]
            + taps_ref[i, 2:3, at] * wide[HALO - 2 : HALO - 2 + tokens]
        )

    signal_cross = [cross(signal_t, signal_strip, signal_hop, dy) for dy in nearest]
    for dy, copy in zip(nearest + [0], signal_cross + [None]):
        at = rows_of(lax.rem(y + dy, ys) * LINE, LINE)
        signal = (shortened(1, at) * shortened(2, at)).astype(bf16)
        signal_ref[:, at] = signal
        signal_t[at, :] = signal.astype(f32).T.astype(bf16)
        if copy is not None:
            copy.start()
    along(signal_t, y * LINE, x_ref, signal_sem, y, 0)

    def query(i, carry):
        at = chunk_at(i)
        query_ref[:, at] = shortened(0, at)
        return carry

    lax.fori_loop(0, chunks, query, 0)

    def pass_signal(index, core):
        dy = nearest[index]
        if core == 0:
            signal_cross[index].wait_recv()
        along(signal_strip.at[dy - 1], 0, x_ref, signal_sem, lax.rem(y + ys - dy, ys), core)

    for index in range(ys - 2):
        pass_signal(index, 0)

    def pass_filter(i, carry):
        origin = lax.rem(spot + LINE - i, LINE)
        pltpu.make_async_remote_copy(
            filter_line.at[i],
            filter_line.at[i],
            filter_send.at[0],
            filter_recv.at[i],
            device_id={"ctx": me},
            device_id_type=MESH,
        ).wait_recv()
        across_filter(filter_line.at[i], origin)
        h_ref[rows_of(y * LINE + origin, 1), :] = filter_line[i, y]
        return carry

    lax.fori_loop(1, LINE, pass_filter, 0)
    pass_signal(ys - 2, 0)
    along(signal_t, y * LINE, x_ref, signal_sem, y, 1)
    for index in range(ys - 1):
        pass_signal(index, 1)

    width = tokens
    first_row = lax.broadcasted_iota(jnp.int32, (blocks, width), 0) == 0
    halves = (slice(0, half_tok), slice(half_tok, tokens))

    def turns_of():
        return twiddle_ref[0, :blocks], twiddle_ref[1, :blocks], twiddle_ref[0, blocks:], twiddle_ref[1, blocks:]

    def spectrum(ref):
        cos, sin, cos_last, sin_last = turns_of()
        for h, part in enumerate(halves):
            wide_ref[h] = ref[:, part].astype(f32)
        turned, last = [], []
        for c in range(lanes):
            picked = pl.ds(c, blocks, stride=lanes)
            column = jnp.concatenate([wide_ref[0, picked, :], wide_ref[1, picked, :]], axis=1).astype(bf16)
            first = dot(lead_ref[...], column)
            real, imag = first[:blocks], first[blocks:]
            last.append(imag[0:1])
            imag = jnp.where(first_row, 0.0, imag)
            turned.append(jnp.concatenate([real * cos - imag * sin, real * sin + imag * cos], axis=1).astype(bf16))
        last = jnp.concatenate(last, axis=0)
        turned.append(jnp.concatenate([last * cos_last, last * sin_last], axis=1).astype(bf16))
        return dot(jnp.concatenate(turned, axis=0), forward_ref[...])

    for load in loads[2:5]:
        load.wait()
    from_filter = settled(x_ref, h_ref, filter_sem, (ys - 1) * LINE)
    from_filter.wait_recv()

    sh_ref[...] = spectrum(h_ref).astype(bf16)
    for load in loads[5:]:
        load.wait()
    from_filter.wait_send()
    sent = pl.ds(0, LINE - 1)
    pltpu.make_async_remote_copy(
        filter_line.at[sent],
        filter_line.at[sent],
        filter_send.at[0],
        filter_recv.at[0],
        device_id={"ctx": me},
        device_id_type=MESH,
    ).wait_send()
    from_signal = settled(signal_t, x_ref, signal_sem, ys * (LINE - 1))
    from_signal.wait_recv()

    sx = spectrum(x_ref)
    xr, xi = sx[:, :width], sx[:, width:]
    hr, hi = sh_ref[:, :width].astype(f32), sh_ref[:, width:].astype(f32)
    product = jnp.concatenate([xr * hr - xi * hi, xr * hi + xi * hr], axis=1).astype(bf16)
    cos, sin, cos_last, sin_last = turns_of()

    def invert(h):
        part = halves[h]
        back = dot(product, backward_ref[:, h * tokens : (h + 1) * tokens])
        br, bi = back[:, :half_tok], back[:, half_tok:]
        last = br[lanes * blocks :] * cos_last[:, part] + bi[lanes * blocks :] * sin_last[:, part]
        for c in range(lanes):
            at = slice(c * blocks, (c + 1) * blocks)
            real, imag = br[at], bi[at]
            imag_turned = jnp.where(first_row[:, part], last[c : c + 1], imag * cos[:, part] - real * sin[:, part])
            turned = jnp.concatenate([real * cos[:, part] + imag * sin[:, part], imag_turned], axis=0).astype(bf16)
            wide_ref[h, pl.ds(c, blocks, stride=lanes), :] = dot(tail_ref[...], turned)
        y_ref[h] = wide_ref[h].astype(bf16)

    waves = ((1, LINE + 1), (LINE + 1, blocks))

    def send_conv(h):
        for wave, (start, stop) in enumerate(waves):

            def one(i, carry, slot=2 * h + wave):
                p = lax.rem(me + i, blocks)
                pltpu.make_async_remote_copy(
                    piece(y_ref.at[h], p),
                    piece(conv_ref.at[h], me),
                    conv_send.at[slot],
                    conv_recv.at[slot],
                    device_id={"ctx": p},
                    device_id_type=MESH,
                ).start()
                return carry

            lax.fori_loop(start, stop, one, 0)

    invert(0)
    send_conv(0)
    invert(1)
    from_conv = []
    for h in range(2):
        conv_ref[h, own, :] = y_ref[h, own, :]
        for wave, (start, stop) in enumerate(waves):
            some = pl.ds(0, (stop - start) * lanes)
            from_conv.append(
                pltpu.make_async_remote_copy(
                    y_ref.at[h, some],
                    conv_ref.at[h, some],
                    conv_send.at[2 * h + wave],
                    conv_recv.at[2 * h + wave],
                    device_id={"ctx": me},
                    device_id_type=MESH,
                )
            )

    def tp_copy(src, dst, h, kind, side):
        s = (h * 3 + kind) * 2 + side
        return pltpu.make_async_remote_copy(
            src, dst, tp_send.at[s], tp_recv.at[s], device_id={"tp": (right, left)[side]}, device_id_type=MESH
        )

    def project(h, dest, start):
        at = pl.ds(pl.multiple_of(dest * cols + start, half_col), half_col)
        return dot(gated_ref[h], weight_ref[:, at])

    far = lax.rem(col + 2, tps)
    relays, opens, sums = {}, {}, {}

    def gate(h):
        tok = pl.ds(h * half_tok, half_tok)
        for i in range(chunks):
            at = slice(i * LANE, (i + 1) * LANE)
            conv = conv_ref[h, at, :].astype(f32).T
            signal = signal_ref[tok, at].astype(f32)
            gated_ref[h, :, at] = (query_ref[tok, at] * (conv + skip_ref[:, at] * signal)).astype(bf16)

    def relay(h):
        for side in range(2):
            relay_src[h, side] = project(h, far, side * half_col).astype(bf16)
            relays[h, side] = tp_copy(relay_src.at[h, side], relay_in.at[h, side], h, 0, side)
            relays[h, side].start()

    def give(h):
        for side, dest in ((0, right), (1, left)):
            send_ref[h, side, 1] = project(h, dest, (1 - side) * half_col).astype(bf16)
            opens[h, side] = tp_copy(send_ref.at[h, side, 1], take_ref.at[h, side, 1], h, 1, side)
            opens[h, side].start()

    def meet(h):
        for side, dest in ((0, right), (1, left)):
            part_ref[h, side] = project(h, dest, side * half_col)

    def add(h):
        for side in range(2):
            relays[h, side].wait_recv()
            send_ref[h, side, 0] = (part_ref[h, side] + relay_in[h, side].astype(f32)).astype(bf16)
            sums[h, side] = tp_copy(send_ref.at[h, side, 0], take_ref.at[h, side, 0], h, 2, side)
            sums[h, side].start()

    def keep(h):
        for part in range(2):
            part_ref[h, 2 + part] = project(h, col, part * half_col)

    for h in range(2):
        from_conv[2 * h].wait_recv()
        if h == 0:
            send_conv(1)
        from_conv[2 * h + 1].wait_recv()
        gate(h)
        relay(h)
        give(h)
        meet(h)
        add(h)
        keep(h)

    for h in range(2):
        for side in range(2):
            opens[h, side].wait_recv()
            sums[h, side].wait_recv()
        tok = pl.ds(h * half_tok, half_tok)
        for part in range(2):
            total = (
                part_ref[h, 2 + part]
                + take_ref[h, 0, part].astype(f32)
                + take_ref[h, 1, 1 - part].astype(f32)
            )
            out_ref[tok, pl.ds(part * half_col, half_col)] = total.astype(bf16)

    from_signal.wait_send()
    for copy in [*signal_cross, *from_conv, *relays.values(), *opens.values(), *sums.values()]:
        copy.wait_send()


def body(qkv, short_taps, long_filter, skip, out_weight):
    blocks = lax.axis_size("ctx")
    tps = lax.axis_size("tp")
    tokens, channels = qkv.shape[1:]
    lanes = channels // blocks
    lines = blocks // LINE
    cols = out_weight.shape[1] // tps
    consts = [jnp.asarray(c) for c in tables(blocks, tokens, lanes)]
    freqs = (blocks + 1) * lanes
    vmem = pl.BlockSpec(memory_space=pltpu.VMEM)
    hbm = pl.BlockSpec(memory_space=pl.ANY)
    bf16 = jnp.bfloat16
    f32 = jnp.float32
    dma = pltpu.SemaphoreType.DMA
    half = tokens // 2
    return pl.pallas_call(
        functools.partial(kernel, blocks, tps, lanes),
        out_shape=pltpu.VMEM((tokens, cols), bf16),
        in_specs=[hbm, vmem, hbm, vmem] + [hbm] * 6,
        out_specs=vmem,
        scratch_shapes=[
            pltpu.VMEM(qkv.shape, bf16),
            pltpu.VMEM((tokens, channels), bf16),
            pltpu.VMEM(out_weight.shape, bf16),
            *[pltpu.VMEM(c.shape, c.dtype) for c in consts],
            pltpu.VMEM((3, HALO, channels), bf16),
            pltpu.VMEM((lines, LINE, lanes, tokens), bf16),
            pltpu.VMEM((channels, tokens), bf16),
            pltpu.VMEM((LINE, lines, lanes, tokens), bf16),
            pltpu.VMEM((lines - 1, LINE * lanes, tokens), bf16),
            pltpu.VMEM((tokens, channels), bf16),
            pltpu.VMEM((tokens, channels), f32),
            pltpu.VMEM((channels, tokens), bf16),
            pltpu.VMEM((channels, tokens), bf16),
            pltpu.VMEM((freqs, 2 * tokens), bf16),
            pltpu.VMEM((2, channels, half), f32),
            pltpu.VMEM((2, channels, half), bf16),
            pltpu.VMEM((2, channels, half), bf16),
            pltpu.VMEM((2, half, channels), bf16),
            pltpu.VMEM((2, 2, half, cols // 2), bf16),
            pltpu.VMEM((2, 2, half, cols // 2), bf16),
            pltpu.VMEM((2, 4, half, cols // 2), f32),
            pltpu.VMEM((2, 2, 2, half, cols // 2), bf16),
            pltpu.VMEM((2, 2, 2, half, cols // 2), bf16),
            dma((8,)),
            dma((2,)),
            dma((1,)),
            dma((LINE,)),
            dma((2, lines - 1)),
            dma((2,)),
            dma((2,)),
            dma((4,)),
            dma((4,)),
            dma((12,)),
            dma((12,)),
        ],
        compiler_params=pltpu.CompilerParams(
            collective_id=0, has_side_effects=True, vmem_limit_bytes=56 << 20
        ),
        name="hyena",
    )(qkv, short_taps, long_filter, skip[None, :], out_weight, *consts)


def solution(mesh):
    placed = (P(None, "ctx", "tp"), P(None, None, "tp"), P("ctx", "tp"), P("tp"), P("tp", None))
    return jax.shard_map(body, mesh=mesh, in_specs=placed, out_specs=P("ctx", "tp"), check_vma=False)
```
